32 devices in a mesh: leaf: 16 (over z, y, core), node: 2 (over x).
Axes of the slice: x: 2, y: 2, z: 4, core: 2. Of those that a mesh axis runs over, the one named last changes fastest.
Arguments:
- leaf_rhs: bfloat16 [16, 2048, 128], P('leaf', 'node'), may hold values from -6 to 6
- leaf_inverse: bfloat16 [16, 2048, 8192], P('leaf', 'node'), as said below
- leaf_update: bfloat16 [16, 1536, 2048], P('leaf', None, 'node'), may hold values from -0.0625 to 0.0625
- root_tiles: int32 [4, 12], replicated, may hold values from 0 to 23, all different within a row
- leaf_dinv: float32 [16, 2048], P('leaf', 'node'), may hold values from 0.5 to 2
- leaf_doff: float32 [16, 1024], P('leaf', 'node'), may hold values from -0.5 to 0.5
- leaf_pairs: int32 [16, 1024], P('leaf', 'node'), may hold values 0 or 1
- root_rhs: bfloat16 [3072, 128], P(('leaf', 'node')), may hold values from -6 to 6
- root_inverse: bfloat16 [3072, 3072], P(('leaf', 'node')), as said below
- root_dinv: float32 [3072], P(('leaf', 'node')), may hold values from 0.5 to 2
- root_doff: float32 [1536], P(('leaf', 'node')), may hold values from -0.5 to 0.5
- root_pairs: int32 [1536], P(('leaf', 'node')), may hold values 0 or 1
Outputs:
- leaf_solution: bfloat16 [16, 2048, 128], P('leaf', 'node')
- root_solution: bfloat16 [3072, 128], P(('leaf', 'node'))
The draws below stay inside these ranges and needn't reach their ends.
Inputs may be any that keep to these rules, and one draw needn't show every extreme that they name: `leaf_inverse`: the 4 row blocks of each leaf, stacked, form Q M transpose(Q) for a permutation matrix Q and a unit lower triangular matrix M. root_inverse is unit lower triangular. `root_tiles`: the 12 tiles of one leaf are distinct, and every root tile is named by some leaf.
All inputs are finite; a program needn't handle non-finite values. No bound on the sum of `leaf_pairs` or of `root_pairs` on one device may be relied on, other than what follows from the above.
Results may differ from the reference program's by a relative error of at most 0.013.
Values may be sent and summed in bfloat16 or wider, within the bound.
A program may use at most 64 MiB of HBM per device.

```python
import math
import jax
import jax.numpy as jnp
from jax import lax

LEAF_ROWS = 8192
RHS = 128
LEAVES = 4
ROOT_TILES = 24
LEAF_TILES = 12
SPLIT = 4
ROOT_ROWS = 3072


def unit_lower(key, shape, order):
    noise = jax.random.normal(key, shape, jnp.float32)
    lower = jnp.tril(noise * (0.5 / math.sqrt(order)), -1) + jnp.eye(order, dtype=jnp.float32)
    return lower


def permuted_leaf(key, index):
    matrix = unit_lower(jax.random.fold_in(key, 2 * index + 1), (LEAF_ROWS, LEAF_ROWS), LEAF_ROWS)
    order_key = jax.random.fold_in(key, 2 * index + 2)
    order = jax.random.permutation(order_key, jnp.arange(LEAF_ROWS, dtype=jnp.int32))
    return matrix[order][:, order]


def draw_leaf_inverse(key, part):
    base = jax.random.fold_in(key, 11)
    whole = jnp.stack([permuted_leaf(base, index) for index in range(LEAVES)], 0)
    return whole.astype(jnp.bfloat16).reshape(LEAVES * SPLIT, LEAF_ROWS // SPLIT, LEAF_ROWS)


def draw_root_inverse(key, part):
    return unit_lower(jax.random.fold_in(key, 23), (ROOT_ROWS, ROOT_ROWS), ROOT_ROWS).astype(jnp.bfloat16)


def touch_ends(entries, stream_key, least, high):
    longest = entries.shape.index(max(entries.shape))
    spots = []
    for shift in (0, 1):
        where = [jax.random.randint(jax.random.fold_in(stream_key, axis), (), 0, length) for axis, length in enumerate(entries.shape)]
        where[longest] = (where[longest] + shift) % entries.shape[longest]
        spots.append(tuple(where))
    return entries.at[spots[0]].set(least).at[spots[1]].set(high)


def steps_of(key, shape, split, smallest, high):
    gain = 1.0
    for dim, blocks in split:
        steps = jax.random.uniform(jax.random.fold_in(jax.random.fold_in(key, 6), dim), (blocks,), jnp.float32, smallest / len(split), high / len(split))
        gain = gain * jnp.repeat(jnp.exp(steps), shape[dim] // blocks).reshape((-1,) + (1,) * (len(shape) - 1 - dim))
    return gain


def different_ones(rng, rows, count, top, lift):
    sequence = jax.random.permutation(jax.random.fold_in(rng, 1), count)
    favour = sequence
    for power in range(3):
        favour = favour * favour // count
    favour = favour * lift // count
    lots = jax.random.randint(jax.random.fold_in(rng, 2), (rows, count), 0, 4096) + favour
    fixed_rows = jax.random.permutation(jax.random.fold_in(rng, 3), rows)[jnp.arange(count) % rows]
    lots = jnp.where(jnp.arange(rows)[:, None] == fixed_rows[None, :], 1 << 14, lots)
    score = lots * count + jnp.arange(count)
    return lax.top_k(score.astype(jnp.int32), top)[1].astype(jnp.int32)


def centred(stream_key, shape, spread, bound, shards=(), kind=jnp.bfloat16):
    entries = spread * jax.random.normal(stream_key, shape, jnp.float32)
    if shards:
        entries = entries * steps_of(stream_key, shape, shards, -0.22, 0.18)
    return jnp.clip(entries, -bound, bound).astype(kind)


def setup_inputs(seed: int = 0) -> dict:
    splits = jax.random.split(jax.random.key(seed), 13)
    return {
        "leaf_rhs": centred(splits[0], (LEAVES * SPLIT, LEAF_ROWS // SPLIT, RHS), 1.0, 6.0, ((0, 16), (1, 2))),
        "leaf_inverse": draw_leaf_inverse(jax.random.fold_in(splits[12], 71), 0),
        "leaf_update": centred(splits[2], (LEAVES * SPLIT, LEAF_TILES * 128, LEAF_ROWS // SPLIT), LEAF_ROWS ** -0.5, 0.0625, ((0, 16), (2, 2))),
        "root_tiles": different_ones(splits[3], LEAVES, ROOT_TILES, LEAF_TILES, 0),
        "leaf_dinv": jnp.clip(jnp.exp(math.log(2.0) - 1.3862944 * jax.random.uniform(splits[4], (LEAVES * SPLIT, LEAF_ROWS // SPLIT), jnp.float32) ** steps_of(splits[4], (LEAVES * SPLIT, LEAF_ROWS // SPLIT), ((0, 16), (1, 2)), -0.2, 0.2)), 0.5, 2.0),
        "leaf_doff": jnp.clip(jax.random.uniform(splits[5], (LEAVES * SPLIT, LEAF_ROWS // (2 * SPLIT)), jnp.float32, -0.5, 0.5) * steps_of(splits[5], (LEAVES * SPLIT, LEAF_ROWS // (2 * SPLIT)), ((0, 16), (1, 2)), -0.4, 0.0), -0.5, 0.5),
        "leaf_pairs": touch_ends((jax.random.randint(splits[6], (LEAVES * SPLIT, LEAF_ROWS // (2 * SPLIT)), 0, 2) < 1).astype(jnp.int32), jax.random.fold_in(splits[6], 1), 0, 1),
        "root_rhs": centred(splits[7], (ROOT_ROWS, RHS), 1.0, 6.0, ((0, 32),)),
        "root_inverse": draw_root_inverse(jax.random.fold_in(splits[12], 71), 0),
        "root_dinv": jnp.clip(jnp.exp(math.log(2.0) - 1.3862944 * jax.random.uniform(splits[9], (ROOT_ROWS,), jnp.float32) ** steps_of(splits[9], (ROOT_ROWS,), ((0, 32),), -0.2, 0.2)), 0.5, 2.0),
        "root_doff": jnp.clip(jax.random.uniform(splits[10], (ROOT_ROWS // 2,), jnp.float32, -0.5, 0.5) * steps_of(splits[10], (ROOT_ROWS // 2,), ((0, 32),), -0.4, 0.0), -0.5, 0.5),
        "root_pairs": touch_ends((jax.random.randint(splits[11], (ROOT_ROWS // 2,), 0, 2) < 1).astype(jnp.int32), jax.random.fold_in(splits[11], 1), 0, 1),
    }


tile_rows = 128


def pivot_solve(values, diagonal, coupling, pairs):
    length = values.shape[0]
    halves = values.reshape(length // 2, 2, values.shape[1])
    diag_two = diagonal.reshape(length // 2, 2)
    joined = (coupling * pairs.astype(jnp.float32))[:, None]
    first_row = diag_two[:, 0:1] * halves[:, 0, :] + joined * halves[:, 1, :]
    second_row = joined * halves[:, 0, :] + diag_two[:, 1:2] * halves[:, 1, :]
    return jnp.stack([first_row, second_row], axis=1).reshape(length, values.shape[1])


def tile_onehot(tile_ids):
    return (jnp.arange(ROOT_TILES, dtype=jnp.int32)[:, None] == tile_ids[None, :]).astype(jnp.float32)


def reference(leaf_rhs, leaf_inverse, leaf_update, root_tiles, leaf_dinv, leaf_doff, leaf_pairs, root_rhs, root_inverse, root_dinv, root_doff, root_pairs):
    full_rhs = leaf_rhs.reshape(LEAVES, LEAF_ROWS, RHS)
    full_inverse = leaf_inverse.reshape(LEAVES, LEAF_ROWS, LEAF_ROWS)
    full_update = leaf_update.reshape(LEAVES, SPLIT, LEAF_TILES * tile_rows, LEAF_ROWS // SPLIT)
    full_update = jnp.transpose(full_update, (0, 2, 1, 3)).reshape(LEAVES, LEAF_TILES * tile_rows, LEAF_ROWS)
    full_dinv = leaf_dinv.reshape(LEAVES, LEAF_ROWS)
    full_doff = leaf_doff.reshape(LEAVES, LEAF_ROWS // 2)
    full_pairs = leaf_pairs.reshape(LEAVES, LEAF_ROWS // 2)

    def forward_step(total, items):
        right, factor, update, tile_ids = items
        forward = jnp.dot(factor, right, preferred_element_type=jnp.float32).astype(jnp.bfloat16)
        update_term = jnp.dot(update, forward, preferred_element_type=jnp.float32)
        placed = jnp.einsum("tk,kar->tar", tile_onehot(tile_ids), update_term.reshape(LEAF_TILES, tile_rows, RHS), precision=lax.Precision.HIGHEST)
        return total + placed.reshape(ROOT_ROWS, RHS), forward

    gathered, leaf_forward = lax.scan(forward_step, jnp.zeros((ROOT_ROWS, RHS), jnp.float32), (full_rhs, full_inverse, full_update, root_tiles))
    root_reduced = (root_rhs.astype(jnp.float32) - gathered).astype(jnp.bfloat16)
    root_forward = jnp.dot(root_inverse, root_reduced, preferred_element_type=jnp.float32)
    root_scaled = pivot_solve(root_forward, root_dinv, root_doff, root_pairs).astype(jnp.bfloat16)
    root_solution = jnp.dot(root_inverse.T, root_scaled, preferred_element_type=jnp.float32).astype(jnp.bfloat16)
    root_blocks = root_solution.astype(jnp.float32).reshape(ROOT_TILES, tile_rows, RHS)

    def backward_step(items):
        forward, factor, update, tile_ids, diagonal, coupling, pairs = items
        tile_values = jnp.einsum("tk,tar->kar", tile_onehot(tile_ids), root_blocks, precision=lax.Precision.HIGHEST)
        tile_values = tile_values.reshape(LEAF_TILES * tile_rows, RHS).astype(jnp.bfloat16)
        scaled = pivot_solve(forward.astype(jnp.float32), diagonal, coupling, pairs)
        leaf_vector = (scaled - jnp.dot(update.T, tile_values, preferred_element_type=jnp.float32)).astype(jnp.bfloat16)
        return jnp.dot(factor.T, leaf_vector, preferred_element_type=jnp.float32).astype(jnp.bfloat16)

    leaf_solution = lax.map(backward_step, (leaf_forward, full_inverse, full_update, root_tiles, full_dinv, full_doff, full_pairs))
    return leaf_solution.reshape(LEAVES * SPLIT, LEAF_ROWS // SPLIT, RHS), root_solution
```

```python
import functools

import jax
import jax.numpy as jnp
from jax import lax
from jax.experimental import pallas as pl
from jax.experimental.pallas import tpu as pltpu
from jax.sharding import PartitionSpec as P

LEAVES = 4
ROOT_TILES = 24


tile_rows = 128


def partner(value, axis, apart):
    mask = 2**apart
    pairs = [(source, source ^ mask) for source in range(lax.axis_size(axis))]
    return lax.ppermute(value, axis, pairs)


def pivot_solve(values, diagonal, coupling, pairs):
    length = values.shape[0]
    halves = values.reshape(length // 2, 2, values.shape[1])
    diag_two = diagonal.reshape(length // 2, 2)
    joined = (coupling * pairs.astype(jnp.float32))[:, None]
    first_row = diag_two[:, 0:1] * halves[:, 0, :] + joined * halves[:, 1, :]
    second_row = joined * halves[:, 0, :] + diag_two[:, 1:2] * halves[:, 1, :]
    return jnp.stack([first_row, second_row], axis=1).reshape(length, values.shape[1])


def transposed_product(matrix, vector):
    return lax.dot_general(
        matrix, vector, (((0,), (0,)), ((), ())), preferred_element_type=jnp.float32
    )


def on_device(
    leaf_rhs,
    leaf_inverse,
    leaf_update,
    root_tiles,
    leaf_dinv,
    leaf_doff,
    leaf_pairs,
    root_rhs,
    root_inverse,
    root_dinv,
    root_doff,
    root_pairs,
):
    factor_rows = leaf_inverse[0]
    local_rows = factor_rows.shape[0]
    rhs_count = leaf_rhs.shape[2]
    root_local = root_rhs.shape[0]
    group_size = lax.axis_size("leaf") // LEAVES
    node_count = lax.axis_size("node")
    bit_count = group_size.bit_length() - 1
    leaf_index = lax.axis_index("leaf")
    group_member = leaf_index % group_size
    leaf_owner = leaf_index // group_size
    block_rows = node_count * local_rows
    holding = lax.all_gather(leaf_rhs[0], "node", axis=0, tiled=True)
    block_start = group_member * block_rows
    own_columns = lax.dynamic_slice_in_dim(factor_rows, block_start, block_rows, 1)
    product_sum = jnp.dot(own_columns, holding, preferred_element_type=jnp.float32)
    for bit_number in range(bit_count):
        partner_rows = partner(holding, "leaf", bit_number)
        span_rows = holding.shape[0]
        partner_start = (group_member >> bit_number ^ 1) * span_rows
        columns = lax.dynamic_slice_in_dim(factor_rows, partner_start, span_rows, 1)
        product_sum = product_sum + jnp.dot(
            columns, partner_rows, preferred_element_type=jnp.float32
        )
        if bit_number + 1 < bit_count:
            low_side = group_member >> bit_number & 1 == 0
            holding = jnp.where(
                low_side,
                jnp.concatenate([holding, partner_rows], 0),
                jnp.concatenate([partner_rows, holding], 0),
            )
    leaf_forward = product_sum.astype(jnp.bfloat16)
    update_rows = leaf_update[0]
    tile_ids = lax.dynamic_index_in_dim(root_tiles, leaf_owner, 0, keepdims=False)
    tile_count = tile_ids.shape[0]
    onehot = (jnp.arange(ROOT_TILES, dtype=jnp.int32)[:, None] == tile_ids[None, :]).astype(
        jnp.float32
    )
    update_term = jnp.dot(update_rows, leaf_forward, preferred_element_type=jnp.float32)
    scattered = jnp.einsum(
        "tk,kar->tar",
        onehot,
        update_term.reshape(tile_count, tile_rows, rhs_count),
        precision=lax.Precision.HIGHEST,
    )
    scattered = scattered.reshape(ROOT_TILES * tile_rows, rhs_count)
    offset = lax.axis_index(("leaf", "node")) * root_local
    own_rows = lax.dynamic_update_slice_in_dim(
        jnp.zeros_like(scattered), root_rhs.astype(jnp.float32), offset, 0
    )
    merged = lax.psum(own_rows - scattered, ("leaf", "node")).astype(jnp.bfloat16)
    root_forward = jnp.dot(root_inverse, merged, preferred_element_type=jnp.float32)
    root_scaled = pivot_solve(root_forward, root_dinv, root_doff, root_pairs).astype(jnp.bfloat16)
    full_term = transposed_product(root_inverse, root_scaled)
    root_full = lax.psum(full_term, ("leaf", "node")).astype(jnp.bfloat16)
    own_offset = lax.axis_index(("leaf", "node")) * root_local
    root_own = lax.dynamic_slice_in_dim(root_full, own_offset, root_local, 0)
    tile_values = jnp.einsum(
        "tk,tar->kar",
        onehot.astype(jnp.bfloat16),
        root_full.reshape(ROOT_TILES, tile_rows, rhs_count),
        preferred_element_type=jnp.float32,
    )
    tile_values = tile_values.astype(jnp.bfloat16).reshape(tile_count * tile_rows, rhs_count)
    coupling_term = transposed_product(update_rows, tile_values)
    leaf_scaled = pivot_solve(
        leaf_forward.astype(jnp.float32), leaf_dinv[0], leaf_doff[0], leaf_pairs[0]
    )
    leaf_vector = (leaf_scaled - coupling_term).astype(jnp.bfloat16)
    back_term = transposed_product(factor_rows, leaf_vector)
    for bit_number in reversed(range(bit_count)):
        half_rows = back_term.shape[0] // 2
        lower_rows = back_term[:half_rows]
        upper_rows = back_term[half_rows:]
        high_side = group_member >> bit_number & 1 == 1
        outgoing = jnp.where(high_side, lower_rows, upper_rows)
        keeping = jnp.where(high_side, upper_rows, lower_rows)
        back_term = keeping + partner(outgoing.astype(jnp.bfloat16), "leaf", bit_number).astype(
            outgoing.dtype
        )
    leaf_solution = lax.psum_scatter(
        back_term.astype(jnp.bfloat16), "node", scatter_dimension=0, tiled=True
    )
    return (leaf_solution[None], root_own)


def flipped(value, mask):
    bit = 1
    while bit <= mask:
        if mask & bit:
            value = value + bit - 2 * bit * lax.rem(lax.div(value, bit), 2)
        bit *= 2
    return value


def column_of(row, group):
    count = row.shape[1]
    length = -(-count * group // tile_rows) * tile_rows
    shape = (length, count)
    place = lax.broadcasted_iota(jnp.int32, shape, 0)
    if group > 1:
        place = lax.div(place, group)
    lane = lax.broadcasted_iota(jnp.int32, shape, 1)
    return jnp.sum(jnp.where(place == lane, row, 0.0), axis=1, keepdims=True)


def paired(values, diagonal, joined):
    length = values.shape[0]
    odd = lax.rem(lax.broadcasted_iota(jnp.int32, values.shape, 0), 2) == 1
    other = jnp.where(odd, pltpu.roll(values, 1, 0), pltpu.roll(values, length - 1, 0))
    return diagonal * values + joined * other


def solve_kernel(
    leaves,
    group_size,
    node_count,
    rhs_hbm,
    inverse_hbm,
    update_hbm,
    tiles,
    dinv,
    doff,
    pairs,
    root_rhs,
    root_inv_hbm,
    root_dinv,
    root_doff,
    root_pairs,
    leaf_out,
    root_out,
    right,
    inverse,
    update,
    root_inv,
    total,
    forward,
    term,
    scaled_t,
    vector_t,
    values_t,
    whole_t,
    scattered,
    near_out,
    near_in,
    far_out,
    far_in,
    deep_out,
    deep_in,
    reduced,
    back_keep,
    back_near_out,
    back_near_in,
    back_far_out,
    back_far_in,
    load_sem,
    right_send,
    right_recv,
    sum_send,
    sum_recv,
    spread_send,
    spread_recv,
    back_send,
    back_recv,
):
    f32, bf16 = jnp.float32, jnp.bfloat16
    leaf = lax.axis_index("leaf")
    node = lax.axis_index("node")
    owner = lax.div(leaf, group_size)
    member = lax.rem(leaf, group_size) * node_count + node
    members = group_size * node_count
    sib = node_count
    cross = sorted((d for d in range(1, members) if not d & sib), key=lambda d: -bin(d).count("1"))
    local = rhs_hbm.shape[1]
    own_rows = root_rhs.shape[0]
    band = members * own_rows
    band_tiles = band // tile_rows
    step = 2 * tile_rows
    pending = []

    def peer(d):
        return flipped(leaf, d // node_count), flipped(node, d % node_count)

    def level(dz):
        other = lax.rem(owner + dz, leaves)
        return other, (lax.rem(leaf + dz * group_size, leaves * group_size), node)

    def send(source, target, send_sem, recv_sem, device):
        copy = pltpu.make_async_remote_copy(
            src_ref=source,
            dst_ref=target,
            send_sem=send_sem,
            recv_sem=recv_sem,
            device_id=device,
            device_id_type=pl.DeviceIdType.MESH,
        )
        copy.start()
        pending.append(copy)
        return copy

    order = [0, sib] + cross[::-1] + [d + sib for d in cross[::-1]]
    loads = {}
    for d in order:
        start = pl.multiple_of(flipped(member, d) * local, tile_rows)
        loads[d] = pltpu.make_async_copy(
            inverse_hbm.at[0, :, pl.ds(start, local)], inverse.at[d], load_sem.at[d]
        )
    own_load = pltpu.make_async_copy(rhs_hbm.at[0], right.at[0], load_sem.at[members])
    update_load = pltpu.make_async_copy(update_hbm.at[0], update, load_sem.at[members + 1])
    root_load = pltpu.make_async_copy(
        root_inv_hbm, root_inv.at[pl.ds(0, own_rows)], load_sem.at[members + 2]
    )
    own_load.start()
    for d in order:
        loads[d].start()
    update_load.start()
    root_load.start()

    near = [sib] + cross
    barrier = pltpu.get_barrier_semaphore()
    for d in near:
        pl.semaphore_signal(
            barrier, inc=1, device_id=peer(d), device_id_type=pl.DeviceIdType.MESH
        )
    for dz in range(1, leaves):
        pl.semaphore_signal(
            barrier, inc=1, device_id=level(dz)[1], device_id_type=pl.DeviceIdType.MESH
        )
    pl.semaphore_wait(barrier, len(near) + leaves - 1)

    arrivals = {}
    for d in cross + [sib]:
        arrivals[d] = send(
            rhs_hbm.at[0], right.at[d], right_send.at[d], right_recv.at[d], peer(d)
        )
    total[...] = jnp.zeros_like(total)
    if root_inv.shape[0] > own_rows:
        root_inv[own_rows:, :] = jnp.zeros(
            (root_inv.shape[0] - own_rows, root_inv.shape[1]), bf16
        )

    def product(d):
        loads[d].wait()

        @pl.loop(0, local // step)
        def _(i):
            rows = pl.ds(pl.multiple_of(i * step, step), step)
            total[rows, :] += jnp.dot(
                inverse[d, rows, :], right[d], preferred_element_type=f32
            )

    def relay(d):
        arrivals[d].wait_recv()
        arrivals[d + sib] = send(
            right.at[d],
            right.at[d + sib],
            right_send.at[d + sib],
            right_recv.at[d + sib],
            peer(sib),
        )

    own_load.wait()
    product(0)
    arrivals[sib].wait_recv()
    product(sib)
    for d in cross[::-1][:-1]:
        relay(d)
    for d in cross[::-1][:-1]:
        product(d)
    relay(cross[0])
    product(cross[0])
    for d in cross[::-1]:
        arrivals[d + sib].wait_recv()
        product(d + sib)
    forward[...] = total[...].astype(bf16)

    update_load.wait()
    tile_count = update.shape[0] // tile_rows

    @pl.loop(0, tile_count)
    def _(k):
        rows = pl.ds(pl.multiple_of(k * tile_rows, tile_rows), tile_rows)
        term[k] = jnp.dot(update[rows, :], forward[...], preferred_element_type=f32)

    names = [tiles[owner, k] for k in range(tile_count)]
    for t in range(leaves * band_tiles):
        rows = pl.ds(t % band_tiles * tile_rows, tile_rows)
        placed = jnp.zeros(term.shape[1:], f32)
        for k in range(tile_count):
            placed = jnp.where(names[k] == t, term[k], placed)
        scattered[0, t // band_tiles, rows, :] = placed

    def block_rows(d):
        return pl.ds(pl.multiple_of(flipped(member, d) * own_rows, 16), own_rows)

    spots = {d: i for i, d in enumerate(cross + [0])}

    def sum_all(use, meanwhile):
        first, second = {}, {}
        for d in cross + [0]:
            i = spots[d]
            near_out[use, i] = scattered[use, :, block_rows(d + sib), :].astype(bf16)
            first[d] = send(
                near_out.at[use, i],
                near_in.at[use, i],
                sum_send.at[use, i],
                sum_recv.at[use, i],
                peer(sib),
            )
        base = len(spots)
        for d in cross:
            i = spots[d]
            first[d].wait_recv()
            both = scattered[use, :, block_rows(d), :] + near_in[use, i].astype(f32)
            far_out[use, i] = both.astype(bf16)
            second[d] = send(
                far_out.at[use, i],
                far_in.at[use, i],
                sum_send.at[use, base + i],
                sum_recv.at[use, base + i],
                peer(d),
            )
        meanwhile()
        first[0].wait_recv()
        mine = scattered[use, :, block_rows(0), :] + near_in[use, spots[0]].astype(f32)
        for d in cross:
            second[d].wait_recv()
            mine = mine + far_in[use, spots[d]].astype(f32)
        deep_out[use] = mine.astype(bf16)
        base += len(cross)
        third = []
        for dz in range(1, leaves):
            other, device = level(dz)
            third.append(
                send(
                    deep_out.at[use, other],
                    deep_in.at[use, dz],
                    sum_send.at[use, base + dz],
                    sum_recv.at[use, base + dz],
                    device,
                )
            )
        result = deep_out[use, owner].astype(f32)
        for dz in range(1, leaves):
            third[dz - 1].wait_recv()
            result = result + deep_in[use, dz].astype(f32)
        return result

    def spread(use, value):
        reduced[use, owner, block_rows(0), :] = value
        copies = []
        for dz in range(1, leaves):
            here = reduced.at[use, owner, block_rows(0), :]
            copies.append(
                send(
                    here, here, spread_send.at[use, dz], spread_recv.at[use, dz], level(dz)[1]
                )
            )
        for copy in copies:
            copy.wait_recv()
        base = leaves
        first, second = {}, []
        for d in cross + [sib]:
            here = reduced.at[use, :, block_rows(0), :]
            first[d] = send(
                here, here, spread_send.at[use, base + d], spread_recv.at[use, base + d], peer(d)
            )
        for d in cross[::-1]:
            first[d].wait_recv()
            here = reduced.at[use, :, block_rows(d), :]
            second.append(
                send(
                    here,
                    here,
                    spread_send.at[use, base + d + sib],
                    spread_recv.at[use, base + d + sib],
                    peer(sib),
                )
            )
        first[sib].wait_recv()
        for copy in second:
            copy.wait_recv()

    def scale_leaf():
        for c in range(local // step):
            rows = pl.ds(c * step, step)
            joined = (
                doff[:, pl.ds(c * tile_rows, tile_rows)]
                * pairs[:, pl.ds(c * tile_rows, tile_rows)].astype(f32)
            )
            scaled = paired(
                forward[rows, :].astype(f32), column_of(dinv[:, rows], 1), column_of(joined, 2)
            )
            scaled_t[:, rows] = scaled.T

    gathered = sum_all(0, scale_leaf)
    spread(0, (root_rhs[...].astype(f32) - gathered).astype(bf16))
    root_load.wait()
    root_forward = jnp.zeros((root_inv.shape[0], root_rhs.shape[1]), f32)
    for z in range(leaves):
        root_forward = root_forward + jnp.dot(
            root_inv[:, z * band : (z + 1) * band], reduced[0, z], preferred_element_type=f32
        )
    root_scaled = paired(
        root_forward,
        column_of(root_dinv[...], 1),
        column_of(root_doff[...] * root_pairs[...].astype(f32), 2),
    )
    root_scaled_t = root_scaled.T.astype(bf16)
    for z in range(leaves):
        scattered[1, z] = jnp.dot(
            root_scaled_t, root_inv[:, z * band : (z + 1) * band], preferred_element_type=f32
        ).T
    root_own = sum_all(1, lambda: None).astype(bf16)
    root_out[...] = root_own
    spread(1, root_own)

    for t in range(leaves * band_tiles):
        rows = pl.ds(t % band_tiles * tile_rows, tile_rows)
        whole_t[t] = reduced[1, t // band_tiles, rows, :].astype(f32).T
    for k in range(tile_count):
        values_t[:, k * tile_rows : (k + 1) * tile_rows] = whole_t[names[k]].astype(bf16)

    @pl.loop(0, local // step)
    def _(c):
        rows = pl.ds(pl.multiple_of(c * step, step), step)
        coupled = jnp.dot(values_t[...], update[:, rows], preferred_element_type=f32)
        vector_t[:, rows] = (scaled_t[:, rows] - coupled).astype(bf16)

    def back(d, target):
        @pl.loop(0, local // step)
        def _(c):
            rows = pl.ds(pl.multiple_of(c * step, step), step)
            target[:, rows] = jnp.dot(
                vector_t[...], inverse[d, :, rows], preferred_element_type=f32
            ).astype(target.dtype)

    first, second = {}, {}
    base = len(spots)

    def pass_on(d):
        i = spots[d]
        first[d].wait_recv()
        back_far_out[i] = (back_keep[i] + back_near_in[i].astype(f32)).astype(bf16)
        second[d] = send(
            back_far_out.at[i],
            back_far_in.at[i],
            back_send.at[base + i],
            back_recv.at[base + i],
            peer(d),
        )

    previous = None
    for d in cross + [0]:
        i = spots[d]
        back(d + sib, back_near_out.at[i])
        first[d] = send(
            back_near_out.at[i], back_near_in.at[i], back_send.at[i], back_recv.at[i], peer(sib)
        )
        back(d, back_keep.at[i])
        if previous is not None:
            pass_on(previous)
        previous = d
    first[0].wait_recv()
    i = spots[0]
    result = back_keep[i] + back_near_in[i].astype(f32)
    for d in cross:
        second[d].wait_recv()
        result = result + back_far_in[spots[d]].astype(f32)
    leaf_out[0] = result.T.astype(bf16)
    for copy in pending:
        copy.wait_send()


def in_one_kernel(
    leaf_rhs,
    leaf_inverse,
    leaf_update,
    root_tiles,
    leaf_dinv,
    leaf_doff,
    leaf_pairs,
    root_rhs,
    root_inverse,
    root_dinv,
    root_doff,
    root_pairs,
):
    f32, bf16 = jnp.float32, jnp.bfloat16
    leaves, tile_count = root_tiles.shape
    group_size = lax.axis_size("leaf") // leaves
    node_count = lax.axis_size("node")
    members = group_size * node_count
    local, rhs = leaf_rhs.shape[1:]
    own_rows, root_rows = root_inverse.shape
    band = members * own_rows
    padded = -(-own_rows // tile_rows) * tile_rows
    half = members // 2
    dma = pltpu.SemaphoreType.DMA
    hbm = pl.BlockSpec(memory_space=pl.ANY)
    vmem = pl.BlockSpec(memory_space=pltpu.VMEM)
    smem = pl.BlockSpec(memory_space=pltpu.SMEM)
    flops = 4 * rhs * (local * members * local + tile_count * tile_rows * local)
    return pl.pallas_call(
        functools.partial(solve_kernel, leaves, group_size, node_count),
        out_shape=(
            jax.ShapeDtypeStruct((1, local, rhs), bf16),
            jax.ShapeDtypeStruct((own_rows, rhs), bf16),
        ),
        in_specs=[hbm, hbm, hbm, smem, vmem, vmem, vmem, vmem, hbm, vmem, vmem, vmem],
        out_specs=(vmem, vmem),
        scratch_shapes=[
            pltpu.VMEM((members, local, rhs), bf16),
            pltpu.VMEM((members, local, local), bf16),
            pltpu.VMEM((tile_count * tile_rows, local), bf16),
            pltpu.VMEM((padded, root_rows), bf16),
            pltpu.VMEM((local, rhs), f32),
            pltpu.VMEM((local, rhs), bf16),
            pltpu.VMEM((tile_count, tile_rows, rhs), f32),
            pltpu.VMEM((rhs, local), f32),
            pltpu.VMEM((rhs, local), bf16),
            pltpu.VMEM((rhs, tile_count * tile_rows), bf16),
            pltpu.VMEM((root_rows // tile_rows, rhs, tile_rows), f32),
            pltpu.VMEM((2, leaves, band, rhs), f32),
            pltpu.VMEM((2, half, leaves, own_rows, rhs), bf16),
            pltpu.VMEM((2, half, leaves, own_rows, rhs), bf16),
            pltpu.VMEM((2, half, leaves, own_rows, rhs), bf16),
            pltpu.VMEM((2, half, leaves, own_rows, rhs), bf16),
            pltpu.VMEM((2, leaves, own_rows, rhs), bf16),
            pltpu.VMEM((2, leaves, own_rows, rhs), bf16),
            pltpu.VMEM((2, leaves, band, rhs), bf16),
            pltpu.VMEM((half, rhs, local), f32),
            pltpu.VMEM((half, rhs, local), bf16),
            pltpu.VMEM((half, rhs, local), bf16),
            pltpu.VMEM((half, rhs, local), bf16),
            pltpu.VMEM((half, rhs, local), bf16),
            dma((members + 3,)),
            dma((members,)),
            dma((members,)),
            dma((2, members + leaves)),
            dma((2, members + leaves)),
            dma((2, members + leaves)),
            dma((2, members + leaves)),
            dma((members,)),
            dma((members,)),
        ],
        compiler_params=pltpu.CompilerParams(
            collective_id=0, has_side_effects=True, vmem_limit_bytes=56 * 2**20
        ),
        cost_estimate=pl.CostEstimate(
            flops=flops, bytes_accessed=2 * local * local * members, transcendentals=0
        ),
        name="solve",
    )(
        leaf_rhs,
        leaf_inverse,
        leaf_update,
        root_tiles,
        leaf_dinv,
        leaf_doff,
        leaf_pairs,
        root_rhs,
        root_inverse,
        root_dinv[None],
        root_doff[None],
        root_pairs[None],
    )


def fits_kernel(leaf_rhs, root_tiles, root_rhs, group_size, node_count):
    members = group_size * node_count
    local, own_rows = leaf_rhs.shape[1], root_rhs.shape[0]
    return (
        group_size > 1
        and members & (members - 1) == 0
        and 2 * members * local * local <= 20 * 2**20
        and leaf_rhs.shape[2] == tile_rows
        and local % (2 * tile_rows) == 0
        and own_rows % 16 == 0
        and members * own_rows % tile_rows == 0
    )


def by_shape(*arrays):
    leaf_rhs, root_tiles, root_rhs = arrays[0], arrays[3], arrays[7]
    group_size = lax.axis_size("leaf") // root_tiles.shape[0]
    if fits_kernel(leaf_rhs, root_tiles, root_rhs, group_size, lax.axis_size("node")):
        return in_one_kernel(*arrays)
    return on_device(*arrays)


def solution(mesh):
    in_specs = (
        P("leaf", "node", None),
        P("leaf", "node", None),
        P("leaf", None, "node"),
        P(),
        P("leaf", "node"),
        P("leaf", "node"),
        P("leaf", "node"),
        P(("leaf", "node"), None),
        P(("leaf", "node"), None),
        P(("leaf", "node")),
        P(("leaf", "node")),
        P(("leaf", "node")),
    )
    out_specs = (P("leaf", "node", None), P(("leaf", "node"), None))
    return jax.shard_map(
        by_shape, mesh=mesh, in_specs=in_specs, out_specs=out_specs, check_vma=False
    )
```

```python
import functools

import jax
import jax.numpy as jnp
from jax import lax
from jax.experimental import pallas as pl
from jax.experimental.pallas import tpu as pltpu
from jax.sharding import PartitionSpec as P

LEAVES = 4
ROOT_TILES = 24


tile_rows = 128


def partner(value, axis, apart):
    mask = 2**apart
    pairs = [(source, source ^ mask) for source in range(lax.axis_size(axis))]
    return lax.ppermute(value, axis, pairs)


def pivot_solve(values, diagonal, coupling, pairs):
    length = values.shape[0]
    halves = values.reshape(length // 2, 2, values.shape[1])
    diag_two = diagonal.reshape(length // 2, 2)
    joined = (coupling * pairs.astype(jnp.float32))[:, None]
    first_row = diag_two[:, 0:1] * halves[:, 0, :] + joined * halves[:, 1, :]
    second_row = joined * halves[:, 0, :] + diag_two[:, 1:2] * halves[:, 1, :]
    return jnp.stack([first_row, second_row], axis=1).reshape(length, values.shape[1])


def transposed_product(matrix, vector):
    return lax.dot_general(
        matrix, vector, (((0,), (0,)), ((), ())), preferred_element_type=jnp.float32
    )


def on_device(
    leaf_rhs,
    leaf_inverse,
    leaf_update,
    root_tiles,
    leaf_dinv,
    leaf_doff,
    leaf_pairs,
    root_rhs,
    root_inverse,
    root_dinv,
    root_doff,
    root_pairs,
):
    factor_rows = leaf_inverse[0]
    local_rows = factor_rows.shape[0]
    rhs_count = leaf_rhs.shape[2]
    root_local = root_rhs.shape[0]
    group_size = lax.axis_size("leaf") // LEAVES
    node_count = lax.axis_size("node")
    bit_count = group_size.bit_length() - 1
    leaf_index = lax.axis_index("leaf")
    group_member = leaf_index % group_size
    leaf_owner = leaf_index // group_size
    block_rows = node_count * local_rows
    holding = lax.all_gather(leaf_rhs[0], "node", axis=0, tiled=True)
    block_start = group_member * block_rows
    own_columns = lax.dynamic_slice_in_dim(factor_rows, block_start, block_rows, 1)
    product_sum = jnp.dot(own_columns, holding, preferred_element_type=jnp.float32)
    for bit_number in range(bit_count):
        partner_rows = partner(holding, "leaf", bit_number)
        span_rows = holding.shape[0]
        partner_start = (group_member >> bit_number ^ 1) * span_rows
        columns = lax.dynamic_slice_in_dim(factor_rows, partner_start, span_rows, 1)
        product_sum = product_sum + jnp.dot(
            columns, partner_rows, preferred_element_type=jnp.float32
        )
        if bit_number + 1 < bit_count:
            low_side = group_member >> bit_number & 1 == 0
            holding = jnp.where(
                low_side,
                jnp.concatenate([holding, partner_rows], 0),
                jnp.concatenate([partner_rows, holding], 0),
            )
    leaf_forward = product_sum.astype(jnp.bfloat16)
    update_rows = leaf_update[0]
    tile_ids = lax.dynamic_index_in_dim(root_tiles, leaf_owner, 0, keepdims=False)
    tile_count = tile_ids.shape[0]
    onehot = (jnp.arange(ROOT_TILES, dtype=jnp.int32)[:, None] == tile_ids[None, :]).astype(
        jnp.float32
    )
    update_term = jnp.dot(update_rows, leaf_forward, preferred_element_type=jnp.float32)
    scattered = jnp.einsum(
        "tk,kar->tar",
        onehot,
        update_term.reshape(tile_count, tile_rows, rhs_count),
        precision=lax.Precision.HIGHEST,
    )
    scattered = scattered.reshape(ROOT_TILES * tile_rows, rhs_count)
    offset = lax.axis_index(("leaf", "node")) * root_local
    own_rows = lax.dynamic_update_slice_in_dim(
        jnp.zeros_like(scattered), root_rhs.astype(jnp.float32), offset, 0
    )
    merged = lax.psum(own_rows - scattered, ("leaf", "node")).astype(jnp.bfloat16)
    root_forward = jnp.dot(root_inverse, merged, preferred_element_type=jnp.float32)
    root_scaled = pivot_solve(root_forward, root_dinv, root_doff, root_pairs).astype(jnp.bfloat16)
    full_term = transposed_product(root_inverse, root_scaled)
    root_full = lax.psum(full_term, ("leaf", "node")).astype(jnp.bfloat16)
    own_offset = lax.axis_index(("leaf", "node")) * root_local
    root_own = lax.dynamic_slice_in_dim(root_full, own_offset, root_local, 0)
    tile_values = jnp.einsum(
        "tk,tar->kar",
        onehot.astype(jnp.bfloat16),
        root_full.reshape(ROOT_TILES, tile_rows, rhs_count),
        preferred_element_type=jnp.float32,
    )
    tile_values = tile_values.astype(jnp.bfloat16).reshape(tile_count * tile_rows, rhs_count)
    coupling_term = transposed_product(update_rows, tile_values)
    leaf_scaled = pivot_solve(
        leaf_forward.astype(jnp.float32), leaf_dinv[0], leaf_doff[0], leaf_pairs[0]
    )
    leaf_vector = (leaf_scaled - coupling_term).astype(jnp.bfloat16)
    back_term = transposed_product(factor_rows, leaf_vector)
    for bit_number in reversed(range(bit_count)):
        half_rows = back_term.shape[0] // 2
        lower_rows = back_term[:half_rows]
        upper_rows = back_term[half_rows:]
        high_side = group_member >> bit_number & 1 == 1
        outgoing = jnp.where(high_side, lower_rows, upper_rows)
        keeping = jnp.where(high_side, upper_rows, lower_rows)
        back_term = keeping + partner(outgoing.astype(jnp.bfloat16), "leaf", bit_number).astype(
            outgoing.dtype
        )
    leaf_solution = lax.psum_scatter(
        back_term.astype(jnp.bfloat16), "node", scatter_dimension=0, tiled=True
    )
    return (leaf_solution[None], root_own)


def flipped(value, mask):
    bit = 1
    while bit <= mask:
        if mask & bit:
            value = value + bit - 2 * bit * lax.rem(lax.div(value, bit), 2)
        bit *= 2
    return value


def column_of(row, group):
    count = row.shape[1]
    length = -(-count * group // tile_rows) * tile_rows
    shape = (length, count)
    place = lax.broadcasted_iota(jnp.int32, shape, 0)
    if group > 1:
        place = lax.div(place, group)
    lane = lax.broadcasted_iota(jnp.int32, shape, 1)
    return jnp.sum(jnp.where(place == lane, row, 0.0), axis=1, keepdims=True)


def paired(values, diagonal, joined):
    length = values.shape[0]
    odd = lax.rem(lax.broadcasted_iota(jnp.int32, values.shape, 0), 2) == 1
    other = jnp.where(odd, pltpu.roll(values, 1, 0), pltpu.roll(values, length - 1, 0))
    return diagonal * values + joined * other


def solve_kernel(
    leaves,
    group_size,
    node_count,
    rhs_hbm,
    inverse_hbm,
    update_hbm,
    tiles,
    dinv,
    doff,
    pairs,
    root_rhs,
    root_inv_hbm,
    root_dinv,
    root_doff,
    root_pairs,
    leaf_out,
    root_out,
    right,
    inverse,
    update,
    root_inv,
    total,
    forward,
    term,
    scaled_t,
    vector_t,
    values_t,
    whole_t,
    scattered,
    near_out,
    near_in,
    far_out,
    far_in,
    deep_out,
    deep_in,
    reduced,
    back_keep,
    back_near_out,
    back_near_in,
    back_far_out,
    back_far_in,
    back_relay,
    load_sem,
    right_send,
    right_recv,
    sum_send,
    sum_recv,
    spread_send,
    spread_recv,
    back_send,
    back_recv,
):
    f32, bf16 = jnp.float32, jnp.bfloat16
    leaf = lax.axis_index("leaf")
    node = lax.axis_index("node")
    owner = lax.div(leaf, group_size)
    member = lax.rem(leaf, group_size) * node_count + node
    members = group_size * node_count
    sib = node_count
    cross = sorted((d for d in range(1, members) if not d & sib), key=lambda d: -bin(d).count("1"))
    local = rhs_hbm.shape[1]
    own_rows = root_rhs.shape[0]
    band = members * own_rows
    band_tiles = band // tile_rows
    step = 2 * tile_rows
    pending = []

    def peer(d):
        return flipped(leaf, d // node_count), flipped(node, d % node_count)

    def level(dz):
        other = lax.rem(owner + dz, leaves)
        return other, (lax.rem(leaf + dz * group_size, leaves * group_size), node)

    def send(source, target, send_sem, recv_sem, device):
        copy = pltpu.make_async_remote_copy(
            src_ref=source,
            dst_ref=target,
            send_sem=send_sem,
            recv_sem=recv_sem,
            device_id=device,
            device_id_type=pl.DeviceIdType.MESH,
        )
        copy.start()
        pending.append(copy)
        return copy

    corner, one, two = cross
    order = [0, sib, one, two, one + sib, two + sib, corner, corner + sib]
    loads = {}
    for d in order:
        start = pl.multiple_of(flipped(member, d) * local, tile_rows)
        loads[d] = pltpu.make_async_copy(
            inverse_hbm.at[0, :, pl.ds(start, local)], inverse.at[d], load_sem.at[d]
        )
    own_load = pltpu.make_async_copy(rhs_hbm.at[0], right.at[0], load_sem.at[members])
    update_load = pltpu.make_async_copy(update_hbm.at[0], update, load_sem.at[members + 1])
    root_load = pltpu.make_async_copy(
        root_inv_hbm, root_inv.at[pl.ds(0, own_rows)], load_sem.at[members + 2]
    )
    own_load.start()
    for d in order:
        loads[d].start()
    update_load.start()
    root_load.start()

    near = [sib] + cross
    barrier = pltpu.get_barrier_semaphore()
    for d in near:
        pl.semaphore_signal(
            barrier, inc=1, device_id=peer(d), device_id_type=pl.DeviceIdType.MESH
        )
    for dz in range(1, leaves):
        pl.semaphore_signal(
            barrier, inc=1, device_id=level(dz)[1], device_id_type=pl.DeviceIdType.MESH
        )
    pl.semaphore_wait(barrier, len(near) + leaves - 1)

    arrivals = {}
    for d in (one, two, sib):
        arrivals[d] = send(
            rhs_hbm.at[0], right.at[d], right_send.at[d], right_recv.at[d], peer(d)
        )
    total[...] = jnp.zeros_like(total)
    if root_inv.shape[0] > own_rows:
        root_inv[own_rows:, :] = jnp.zeros(
            (root_inv.shape[0] - own_rows, root_inv.shape[1]), bf16
        )

    def product(d):
        loads[d].wait()

        @pl.loop(0, local // step)
        def _(i):
            rows = pl.ds(pl.multiple_of(i * step, step), step)
            total[rows, :] += jnp.dot(
                inverse[d, rows, :], right[d], preferred_element_type=f32
            )

    def to_sibling(d, rows, slot):
        return send(
            right.at[d, rows],
            right.at[d + sib, rows],
            right_send.at[slot],
            right_recv.at[slot],
            peer(sib),
        )

    own_load.wait()
    product(0)
    arrivals[sib].wait_recv()
    product(sib)
    halves = [pl.ds(0, local // 2), pl.ds(local // 2, local // 2)]
    corner_halves = []
    for d, other, rows, slot in ((one, two, halves[0], corner), (two, one, halves[1], members)):
        arrivals[d].wait_recv()
        corner_halves.append(
            send(
                right.at[d, rows],
                right.at[corner, rows],
                right_send.at[slot],
                right_recv.at[slot],
                peer(other),
            )
        )
        arrivals[d + sib] = to_sibling(d, pl.ds(0, local), d + sib)
    product(one)
    product(two)
    arrivals[one + sib].wait_recv()
    product(one + sib)
    last = []
    for copy, rows, slot in zip(corner_halves, halves, (corner + sib, members + 1)):
        copy.wait_recv()
        last.append(to_sibling(corner, rows, slot))
    arrivals[two + sib].wait_recv()
    product(two + sib)
    product(corner)
    for copy in last:
        copy.wait_recv()
    product(corner + sib)
    forward[...] = total[...].astype(bf16)

    update_load.wait()
    tile_count = update.shape[0] // tile_rows

    @pl.loop(0, tile_count)
    def _(k):
        rows = pl.ds(pl.multiple_of(k * tile_rows, tile_rows), tile_rows)
        term[k] = jnp.dot(update[rows, :], forward[...], preferred_element_type=f32)

    names = [tiles[owner, k] for k in range(tile_count)]
    for t in range(leaves * band_tiles):
        rows = pl.ds(t % band_tiles * tile_rows, tile_rows)
        placed = jnp.zeros(term.shape[1:], f32)
        for k in range(tile_count):
            placed = jnp.where(names[k] == t, term[k], placed)
        scattered[0, t // band_tiles, rows, :] = placed

    def block_rows(d):
        return pl.ds(pl.multiple_of(flipped(member, d) * own_rows, 16), own_rows)

    spots = {d: i for i, d in enumerate(cross + [0])}

    def sum_all(use, meanwhile):
        first, second = {}, {}
        for d in cross + [0]:
            i = spots[d]
            near_out[use, i] = scattered[use, :, block_rows(d + sib), :].astype(bf16)
            first[d] = send(
                near_out.at[use, i],
                near_in.at[use, i],
                sum_send.at[use, i],
                sum_recv.at[use, i],
                peer(sib),
            )
        base = len(spots)
        for d in cross:
            i = spots[d]
            first[d].wait_recv()
            both = scattered[use, :, block_rows(d), :] + near_in[use, i].astype(f32)
            far_out[use, i] = both.astype(bf16)
            second[d] = send(
                far_out.at[use, i],
                far_in.at[use, i],
                sum_send.at[use, base + i],
                sum_recv.at[use, base + i],
                peer(d),
            )
        meanwhile()
        first[0].wait_recv()
        mine = scattered[use, :, block_rows(0), :] + near_in[use, spots[0]].astype(f32)
        for d in cross:
            second[d].wait_recv()
            mine = mine + far_in[use, spots[d]].astype(f32)
        deep_out[use] = mine.astype(bf16)
        base += len(cross)
        third = []
        for dz in range(1, leaves):
            other, device = level(dz)
            third.append(
                send(
                    deep_out.at[use, other],
                    deep_in.at[use, dz],
                    sum_send.at[use, base + dz],
                    sum_recv.at[use, base + dz],
                    device,
                )
            )
        result = deep_out[use, owner].astype(f32)
        for dz in range(1, leaves):
            third[dz - 1].wait_recv()
            result = result + deep_in[use, dz].astype(f32)
        return result

    def spread(use, value):
        reduced[use, owner, block_rows(0), :] = value
        copies = []
        for dz in range(1, leaves):
            here = reduced.at[use, owner, block_rows(0), :]
            copies.append(
                send(
                    here, here, spread_send.at[use, dz], spread_recv.at[use, dz], level(dz)[1]
                )
            )
        for copy in copies:
            copy.wait_recv()
        base = leaves
        first, second = {}, []
        for d in cross + [sib]:
            here = reduced.at[use, :, block_rows(0), :]
            first[d] = send(
                here, here, spread_send.at[use, base + d], spread_recv.at[use, base + d], peer(d)
            )
        for d in cross[::-1]:
            first[d].wait_recv()
            here = reduced.at[use, :, block_rows(d), :]
            second.append(
                send(
                    here,
                    here,
                    spread_send.at[use, base + d + sib],
                    spread_recv.at[use, base + d + sib],
                    peer(sib),
                )
            )
        first[sib].wait_recv()
        for copy in second:
            copy.wait_recv()

    def scale_leaf():
        for c in range(local // step):
            rows = pl.ds(c * step, step)
            joined = (
                doff[:, pl.ds(c * tile_rows, tile_rows)]
                * pairs[:, pl.ds(c * tile_rows, tile_rows)].astype(f32)
            )
            scaled = paired(
                forward[rows, :].astype(f32), column_of(dinv[:, rows], 1), column_of(joined, 2)
            )
            scaled_t[:, rows] = scaled.T

    gathered = sum_all(0, scale_leaf)
    spread(0, (root_rhs[...].astype(f32) - gathered).astype(bf16))
    root_load.wait()
    root_forward = jnp.zeros((root_inv.shape[0], root_rhs.shape[1]), f32)
    for z in range(leaves):
        root_forward = root_forward + jnp.dot(
            root_inv[:, z * band : (z + 1) * band], reduced[0, z], preferred_element_type=f32
        )
    root_scaled = paired(
        root_forward,
        column_of(root_dinv[...], 1),
        column_of(root_doff[...] * root_pairs[...].astype(f32), 2),
    )
    root_scaled_t = root_scaled.T.astype(bf16)
    for z in range(leaves):
        scattered[1, z] = jnp.dot(
            root_scaled_t, root_inv[:, z * band : (z + 1) * band], preferred_element_type=f32
        ).T
    root_own = sum_all(1, lambda: None).astype(bf16)
    root_out[...] = root_own
    spread(1, root_own)

    for t in range(leaves * band_tiles):
        rows = pl.ds(t % band_tiles * tile_rows, tile_rows)
        whole_t[t] = reduced[1, t // band_tiles, rows, :].astype(f32).T
    for k in range(tile_count):
        values_t[:, k * tile_rows : (k + 1) * tile_rows] = whole_t[names[k]].astype(bf16)

    @pl.loop(0, local // step)
    def _(c):
        rows = pl.ds(pl.multiple_of(c * step, step), step)
        coupled = jnp.dot(values_t[...], update[:, rows], preferred_element_type=f32)
        vector_t[:, rows] = (scaled_t[:, rows] - coupled).astype(bf16)

    def back(d, target):
        @pl.loop(0, local // step)
        def _(c):
            rows = pl.ds(pl.multiple_of(c * step, step), step)
            target[:, rows] = jnp.dot(
                vector_t[...], inverse[d, :, rows], preferred_element_type=f32
            ).astype(target.dtype)

    first, later = {}, []
    lanes = halves

    def to_near(d):
        i = spots[d]
        back(d + sib, back_near_out.at[i])
        first[d] = send(
            back_near_out.at[i], back_near_in.at[i], back_send.at[i], back_recv.at[i], peer(sib)
        )

    def join(d):
        i = spots[d]
        first[d].wait_recv()
        back_keep[i] = back_keep[i] + back_near_in[i].astype(f32)

    def to_far(d, part, target, slot, device):
        i = spots[d]
        back_far_out[i, :, lanes[part]] = back_keep[i, :, lanes[part]].astype(bf16)
        return send(
            back_far_out.at[i, :, lanes[part]],
            target,
            back_send.at[slot],
            back_recv.at[slot],
            device,
        )

    base = len(spots)
    to_near(corner)
    back(corner, back_keep.at[spots[corner]])
    to_near(one)
    join(corner)
    relayed = [
        to_far(corner, 0, back_relay.at[0], base, peer(one)),
        to_far(corner, 1, back_relay.at[1], base + 1, peer(two)),
    ]
    back(one, back_keep.at[spots[one]])
    to_near(two)
    join(one)
    later.append(to_far(one, 0, back_far_in.at[0, :, lanes[0]], base + 2, peer(one)))
    back(two, back_keep.at[spots[two]])
    join(two)
    later.append(to_far(two, 1, back_far_in.at[1, :, lanes[1]], base + 3, peer(two)))
    for d, part, place in ((two, 0, 1), (one, 1, 0)):
        i = spots[d]
        relayed[part].wait_recv()
        back_keep[i, :, lanes[part]] = back_keep[i, :, lanes[part]] + back_relay[part].astype(f32)
        later.append(
            to_far(d, part, back_far_in.at[place, :, lanes[part]], base + 4 + part, peer(d))
        )
    to_near(0)
    back(0, back_keep.at[spots[0]])
    join(0)
    for copy in later:
        copy.wait_recv()
    result = back_keep[spots[0]] + back_far_in[0].astype(f32) + back_far_in[1].astype(f32)
    leaf_out[0] = result.T.astype(bf16)
    for copy in pending:
        copy.wait_send()


def in_one_kernel(
    leaf_rhs,
    leaf_inverse,
    leaf_update,
    root_tiles,
    leaf_dinv,
    leaf_doff,
    leaf_pairs,
    root_rhs,
    root_inverse,
    root_dinv,
    root_doff,
    root_pairs,
):
    f32, bf16 = jnp.float32, jnp.bfloat16
    leaves, tile_count = root_tiles.shape
    group_size = lax.axis_size("leaf") // leaves
    node_count = lax.axis_size("node")
    members = group_size * node_count
    local, rhs = leaf_rhs.shape[1:]
    own_rows, root_rows = root_inverse.shape
    band = members * own_rows
    padded = -(-own_rows // tile_rows) * tile_rows
    half = members // 2
    dma = pltpu.SemaphoreType.DMA
    hbm = pl.BlockSpec(memory_space=pl.ANY)
    vmem = pl.BlockSpec(memory_space=pltpu.VMEM)
    smem = pl.BlockSpec(memory_space=pltpu.SMEM)
    flops = 4 * rhs * (local * members * local + tile_count * tile_rows * local)
    return pl.pallas_call(
        functools.partial(solve_kernel, leaves, group_size, node_count),
        out_shape=(
            jax.ShapeDtypeStruct((1, local, rhs), bf16),
            jax.ShapeDtypeStruct((own_rows, rhs), bf16),
        ),
        in_specs=[hbm, hbm, hbm, smem, vmem, vmem, vmem, vmem, hbm, vmem, vmem, vmem],
        out_specs=(vmem, vmem),
        scratch_shapes=[
            pltpu.VMEM((members, local, rhs), bf16),
            pltpu.VMEM((members, local, local), bf16),
            pltpu.VMEM((tile_count * tile_rows, local), bf16),
            pltpu.VMEM((padded, root_rows), bf16),
            pltpu.VMEM((local, rhs), f32),
            pltpu.VMEM((local, rhs), bf16),
            pltpu.VMEM((tile_count, tile_rows, rhs), f32),
            pltpu.VMEM((rhs, local), f32),
            pltpu.VMEM((rhs, local), bf16),
            pltpu.VMEM((rhs, tile_count * tile_rows), bf16),
            pltpu.VMEM((root_rows // tile_rows, rhs, tile_rows), f32),
            pltpu.VMEM((2, leaves, band, rhs), f32),
            pltpu.VMEM((2, half, leaves, own_rows, rhs), bf16),
            pltpu.VMEM((2, half, leaves, own_rows, rhs), bf16),
            pltpu.VMEM((2, half, leaves, own_rows, rhs), bf16),
            pltpu.VMEM((2, half, leaves, own_rows, rhs), bf16),
            pltpu.VMEM((2, leaves, own_rows, rhs), bf16),
            pltpu.VMEM((2, leaves, own_rows, rhs), bf16),
            pltpu.VMEM((2, leaves, band, rhs), bf16),
            pltpu.VMEM((half, rhs, local), f32),
            pltpu.VMEM((half, rhs, local), bf16),
            pltpu.VMEM((half, rhs, local), bf16),
            pltpu.VMEM((half, rhs, local), bf16),
            pltpu.VMEM((2, rhs, local), bf16),
            pltpu.VMEM((2, rhs, local // 2), bf16),
            dma((members + 3,)),
            dma((members + 2,)),
            dma((members + 2,)),
            dma((2, members + leaves)),
            dma((2, members + leaves)),
            dma((2, members + leaves)),
            dma((2, members + leaves)),
            dma((members + 2,)),
            dma((members + 2,)),
        ],
        compiler_params=pltpu.CompilerParams(
            collective_id=0, has_side_effects=True, vmem_limit_bytes=56 * 2**20
        ),
        cost_estimate=pl.CostEstimate(
            flops=flops, bytes_accessed=2 * local * local * members, transcendentals=0
        ),
        name="solve",
    )(
        leaf_rhs,
        leaf_inverse,
        leaf_update,
        root_tiles,
        leaf_dinv,
        leaf_doff,
        leaf_pairs,
        root_rhs,
        root_inverse,
        root_dinv[None],
        root_doff[None],
        root_pairs[None],
    )


def fits_kernel(leaf_rhs, root_tiles, root_rhs, group_size, node_count):
    members = group_size * node_count
    local, own_rows = leaf_rhs.shape[1], root_rhs.shape[0]
    return (
        group_size % 2 == 0
        and members == 8
        and 2 * members * local * local <= 20 * 2**20
        and leaf_rhs.shape[2] == tile_rows
        and local % (2 * tile_rows) == 0
        and own_rows % 16 == 0
        and members * own_rows % tile_rows == 0
    )


def by_shape(*arrays):
    leaf_rhs, root_tiles, root_rhs = arrays[0], arrays[3], arrays[7]
    group_size = lax.axis_size("leaf") // root_tiles.shape[0]
    if fits_kernel(leaf_rhs, root_tiles, root_rhs, group_size, lax.axis_size("node")):
        return in_one_kernel(*arrays)
    return on_device(*arrays)


def solution(mesh):
    in_specs = (
        P("leaf", "node", None),
        P("leaf", "node", None),
        P("leaf", None, "node"),
        P(),
        P("leaf", "node"),
        P("leaf", "node"),
        P("leaf", "node"),
        P(("leaf", "node"), None),
        P(("leaf", "node"), None),
        P(("leaf", "node")),
        P(("leaf", "node")),
        P(("leaf", "node")),
    )
    out_specs = (P("leaf", "node", None), P(("leaf", "node"), None))
    return jax.shard_map(
        by_shape, mesh=mesh, in_specs=in_specs, out_specs=out_specs, check_vma=False
    )
```

```python
import functools

import jax
import jax.numpy as jnp
from jax import lax
from jax.experimental import pallas as pl
from jax.experimental.pallas import tpu as pltpu
from jax.sharding import PartitionSpec as P

LEAVES = 4
ROOT_TILES = 24


tile_rows = 128


def partner(value, axis, apart):
    mask = 2**apart
    pairs = [(source, source ^ mask) for source in range(lax.axis_size(axis))]
    return lax.ppermute(value, axis, pairs)


def pivot_solve(values, diagonal, coupling, pairs):
    length = values.shape[0]
    halves = values.reshape(length // 2, 2, values.shape[1])
    diag_two = diagonal.reshape(length // 2, 2)
    joined = (coupling * pairs.astype(jnp.float32))[:, None]
    first_row = diag_two[:, 0:1] * halves[:, 0, :] + joined * halves[:, 1, :]
    second_row = joined * halves[:, 0, :] + diag_two[:, 1:2] * halves[:, 1, :]
    return jnp.stack([first_row, second_row], axis=1).reshape(length, values.shape[1])


def transposed_product(matrix, vector):
    return lax.dot_general(
        matrix, vector, (((0,), (0,)), ((), ())), preferred_element_type=jnp.float32
    )


def on_device(
    leaf_rhs,
    leaf_inverse,
    leaf_update,
    root_tiles,
    leaf_dinv,
    leaf_doff,
    leaf_pairs,
    root_rhs,
    root_inverse,
    root_dinv,
    root_doff,
    root_pairs,
):
    factor_rows = leaf_inverse[0]
    local_rows = factor_rows.shape[0]
    rhs_count = leaf_rhs.shape[2]
    root_local = root_rhs.shape[0]
    group_size = lax.axis_size("leaf") // LEAVES
    node_count = lax.axis_size("node")
    bit_count = group_size.bit_length() - 1
    leaf_index = lax.axis_index("leaf")
    group_member = leaf_index % group_size
    leaf_owner = leaf_index // group_size
    block_rows = node_count * local_rows
    holding = lax.all_gather(leaf_rhs[0], "node", axis=0, tiled=True)
    block_start = group_member * block_rows
    own_columns = lax.dynamic_slice_in_dim(factor_rows, block_start, block_rows, 1)
    product_sum = jnp.dot(own_columns, holding, preferred_element_type=jnp.float32)
    for bit_number in range(bit_count):
        partner_rows = partner(holding, "leaf", bit_number)
        span_rows = holding.shape[0]
        partner_start = (group_member >> bit_number ^ 1) * span_rows
        columns = lax.dynamic_slice_in_dim(factor_rows, partner_start, span_rows, 1)
        product_sum = product_sum + jnp.dot(
            columns, partner_rows, preferred_element_type=jnp.float32
        )
        if bit_number + 1 < bit_count:
            low_side = group_member >> bit_number & 1 == 0
            holding = jnp.where(
                low_side,
                jnp.concatenate([holding, partner_rows], 0),
                jnp.concatenate([partner_rows, holding], 0),
            )
    leaf_forward = product_sum.astype(jnp.bfloat16)
    update_rows = leaf_update[0]
    tile_ids = lax.dynamic_index_in_dim(root_tiles, leaf_owner, 0, keepdims=False)
    tile_count = tile_ids.shape[0]
    onehot = (jnp.arange(ROOT_TILES, dtype=jnp.int32)[:, None] == tile_ids[None, :]).astype(
        jnp.float32
    )
    update_term = jnp.dot(update_rows, leaf_forward, preferred_element_type=jnp.float32)
    scattered = jnp.einsum(
        "tk,kar->tar",
        onehot,
        update_term.reshape(tile_count, tile_rows, rhs_count),
        precision=lax.Precision.HIGHEST,
    )
    scattered = scattered.reshape(ROOT_TILES * tile_rows, rhs_count)
    offset = lax.axis_index(("leaf", "node")) * root_local
    own_rows = lax.dynamic_update_slice_in_dim(
        jnp.zeros_like(scattered), root_rhs.astype(jnp.float32), offset, 0
    )
    merged = lax.psum(own_rows - scattered, ("leaf", "node")).astype(jnp.bfloat16)
    root_forward = jnp.dot(root_inverse, merged, preferred_element_type=jnp.float32)
    root_scaled = pivot_solve(root_forward, root_dinv, root_doff, root_pairs).astype(jnp.bfloat16)
    full_term = transposed_product(root_inverse, root_scaled)
    root_full = lax.psum(full_term, ("leaf", "node")).astype(jnp.bfloat16)
    own_offset = lax.axis_index(("leaf", "node")) * root_local
    root_own = lax.dynamic_slice_in_dim(root_full, own_offset, root_local, 0)
    tile_values = jnp.einsum(
        "tk,tar->kar",
        onehot.astype(jnp.bfloat16),
        root_full.reshape(ROOT_TILES, tile_rows, rhs_count),
        preferred_element_type=jnp.float32,
    )
    tile_values = tile_values.astype(jnp.bfloat16).reshape(tile_count * tile_rows, rhs_count)
    coupling_term = transposed_product(update_rows, tile_values)
    leaf_scaled = pivot_solve(
        leaf_forward.astype(jnp.float32), leaf_dinv[0], leaf_doff[0], leaf_pairs[0]
    )
    leaf_vector = (leaf_scaled - coupling_term).astype(jnp.bfloat16)
    back_term = transposed_product(factor_rows, leaf_vector)
    for bit_number in reversed(range(bit_count)):
        half_rows = back_term.shape[0] // 2
        lower_rows = back_term[:half_rows]
        upper_rows = back_term[half_rows:]
        high_side = group_member >> bit_number & 1 == 1
        outgoing = jnp.where(high_side, lower_rows, upper_rows)
        keeping = jnp.where(high_side, upper_rows, lower_rows)
        back_term = keeping + partner(outgoing.astype(jnp.bfloat16), "leaf", bit_number).astype(
            outgoing.dtype
        )
    leaf_solution = lax.psum_scatter(
        back_term.astype(jnp.bfloat16), "node", scatter_dimension=0, tiled=True
    )
    return (leaf_solution[None], root_own)


def flipped(value, mask):
    bit = 1
    while bit <= mask:
        if mask & bit:
            value = value + bit - 2 * bit * lax.rem(lax.div(value, bit), 2)
        bit *= 2
    return value


def column_of(row, group):
    count = row.shape[1]
    length = -(-count * group // tile_rows) * tile_rows
    shape = (length, count)
    place = lax.broadcasted_iota(jnp.int32, shape, 0)
    if group > 1:
        place = lax.div(place, group)
    lane = lax.broadcasted_iota(jnp.int32, shape, 1)
    return jnp.sum(jnp.where(place == lane, row, 0.0), axis=1, keepdims=True)


def paired(values, diagonal, joined):
    length = values.shape[0]
    odd = lax.rem(lax.broadcasted_iota(jnp.int32, values.shape, 0), 2) == 1
    other = jnp.where(odd, pltpu.roll(values, 1, 0), pltpu.roll(values, length - 1, 0))
    return diagonal * values + joined * other


def solve_kernel(
    leaves,
    group_size,
    node_count,
    rhs_hbm,
    inverse_hbm,
    update_hbm,
    tiles,
    dinv,
    doff,
    pairs,
    root_rhs,
    root_inv_hbm,
    root_dinv,
    root_doff,
    root_pairs,
    out,
    right,
    inverse,
    update,
    root_inv,
    total,
    forward,
    term,
    scaled_t,
    vector_t,
    values_t,
    whole_t,
    scattered,
    near_out,
    near_in,
    far_out,
    far_in,
    deep_out,
    deep_in,
    reduced,
    back_keep,
    back_near_out,
    back_near_in,
    back_far_out,
    back_far_in,
    back_relay,
    load_sem,
    right_send,
    right_recv,
    sum_send,
    sum_recv,
    spread_send,
    spread_recv,
    back_send,
    back_recv,
):
    f32, bf16 = jnp.float32, jnp.bfloat16
    leaf = lax.axis_index("leaf")
    node = lax.axis_index("node")
    owner = lax.div(leaf, group_size)
    member = lax.rem(leaf, group_size) * node_count + node
    members = group_size * node_count
    sib = node_count
    cross = sorted((d for d in range(1, members) if not d & sib), key=lambda d: -bin(d).count("1"))
    local = rhs_hbm.shape[1]
    own_rows = root_rhs.shape[0]
    band = members * own_rows
    band_tiles = band // tile_rows
    step = 2 * tile_rows
    pending = []

    def peer(d):
        return flipped(leaf, d // node_count), flipped(node, d % node_count)

    def level(dz):
        other = lax.rem(owner + dz, leaves)
        return other, (lax.rem(leaf + dz * group_size, leaves * group_size), node)

    def send(source, target, send_sem, recv_sem, device):
        copy = pltpu.make_async_remote_copy(
            src_ref=source,
            dst_ref=target,
            send_sem=send_sem,
            recv_sem=recv_sem,
            device_id=device,
            device_id_type=pl.DeviceIdType.MESH,
        )
        copy.start()
        pending.append(copy)
        return copy

    corner, one, two = cross
    order = [0, sib, one, two, one + sib, two + sib, corner, corner + sib]
    loads = {}
    for d in order:
        start = pl.multiple_of(flipped(member, d) * local, tile_rows)
        loads[d] = pltpu.make_async_copy(
            inverse_hbm.at[0, :, pl.ds(start, local)], inverse.at[d], load_sem.at[d]
        )
    own_load = pltpu.make_async_copy(rhs_hbm.at[0], right.at[0], load_sem.at[members])
    update_load = pltpu.make_async_copy(update_hbm.at[0], update, load_sem.at[members + 1])
    root_load = pltpu.make_async_copy(
        root_inv_hbm, root_inv.at[pl.ds(0, own_rows)], load_sem.at[members + 2]
    )
    own_load.start()
    for d in order:
        loads[d].start()
    update_load.start()
    root_load.start()

    near = [sib] + cross
    barrier = pltpu.get_barrier_semaphore()
    for d in near:
        pl.semaphore_signal(
            barrier, inc=1, device_id=peer(d), device_id_type=pl.DeviceIdType.MESH
        )
    for dz in range(1, leaves):
        pl.semaphore_signal(
            barrier, inc=1, device_id=level(dz)[1], device_id_type=pl.DeviceIdType.MESH
        )
    pl.semaphore_wait(barrier, len(near) + leaves - 1)

    arrivals = {}
    for d in (one, two, sib):
        arrivals[d] = send(
            rhs_hbm.at[0], right.at[d], right_send.at[d], right_recv.at[d], peer(d)
        )
    total[...] = jnp.zeros_like(total)
    if root_inv.shape[0] > own_rows:
        root_inv[own_rows:, :] = jnp.zeros(
            (root_inv.shape[0] - own_rows, root_inv.shape[1]), bf16
        )

    def product(d):
        loads[d].wait()

        @pl.loop(0, 2)
        def _(i):
            rows = pl.ds(pl.multiple_of(i * (local // 2), tile_rows), local // 2)
            total[rows, :] += jnp.dot(
                inverse[d, rows, :], right[d], preferred_element_type=f32
            )

    def to_sibling(d, rows, slot):
        return send(
            right.at[d, rows],
            right.at[d + sib, rows],
            right_send.at[slot],
            right_recv.at[slot],
            peer(sib),
        )

    own_load.wait()
    product(0)
    arrivals[sib].wait_recv()
    product(sib)
    halves = [pl.ds(0, local // 2), pl.ds(local // 2, local // 2)]
    corner_halves = []
    for d, other, rows, slot in ((one, two, halves[0], corner), (two, one, halves[1], members)):
        arrivals[d].wait_recv()
        corner_halves.append(
            send(
                right.at[d, rows],
                right.at[corner, rows],
                right_send.at[slot],
                right_recv.at[slot],
                peer(other),
            )
        )
        arrivals[d + sib] = to_sibling(d, pl.ds(0, local), d + sib)
    product(one)
    product(two)
    arrivals[one + sib].wait_recv()
    product(one + sib)
    last = []
    for copy, rows, slot in zip(corner_halves, halves, (corner + sib, members + 1)):
        copy.wait_recv()
        last.append(to_sibling(corner, rows, slot))
    arrivals[two + sib].wait_recv()
    product(two + sib)
    product(corner)
    for copy in last:
        copy.wait_recv()
    product(corner + sib)
    forward[...] = total[...].astype(bf16)

    update_load.wait()
    tile_count = update.shape[0] // tile_rows

    batch = 4 if tile_count % 4 == 0 else 1

    @pl.loop(0, tile_count // batch)
    def _(k):
        length = batch * tile_rows
        rows = pl.ds(pl.multiple_of(k * length, length), length)
        product_rows = jnp.dot(update[rows, :], forward[...], preferred_element_type=f32)
        term[pl.ds(k * batch, batch)] = product_rows.reshape(batch, *term.shape[1:])

    names = [tiles[owner, k] for k in range(tile_count)]
    for t in range(leaves * band_tiles):
        rows = pl.ds(t % band_tiles * tile_rows, tile_rows)
        placed = jnp.zeros(term.shape[1:], f32)
        for k in range(tile_count):
            placed = jnp.where(names[k] == t, term[k], placed)
        scattered[0, t // band_tiles, rows, :] = placed

    def block_rows(d):
        return pl.ds(pl.multiple_of(flipped(member, d) * own_rows, 16), own_rows)

    spots = {d: i for i, d in enumerate(cross + [0])}

    def sum_all(use, meanwhile):
        first, second = {}, {}
        for d in cross + [0]:
            i = spots[d]
            near_out[use, i] = scattered[use, :, block_rows(d + sib), :].astype(bf16)
            first[d] = send(
                near_out.at[use, i],
                near_in.at[use, i],
                sum_send.at[use, i],
                sum_recv.at[use, i],
                peer(sib),
            )
        base = len(spots)
        turns = list(range(1, leaves)) + [0]
        for d in cross:
            i = spots[d]
            first[d].wait_recv()
            both = scattered[use, :, block_rows(d), :] + near_in[use, i].astype(f32)
            far_out[use, i] = both.astype(bf16)
            for dz in turns:
                other = level(dz)[0]
                slot = base + i * leaves + dz
                second[d, dz] = send(
                    far_out.at[use, i, other],
                    far_in.at[use, i, other],
                    sum_send.at[use, slot],
                    sum_recv.at[use, slot],
                    peer(d),
                )
        meanwhile()
        first[0].wait_recv()
        base += len(cross) * leaves
        third = []
        for dz in turns:
            other, device = level(dz)
            mine = scattered[use, other, block_rows(0), :]
            mine = mine + near_in[use, spots[0], other].astype(f32)
            for d in cross:
                second[d, dz].wait_recv()
                mine = mine + far_in[use, spots[d], other].astype(f32)
            if dz:
                deep_out[use, dz] = mine.astype(bf16)
                third.append(
                    send(
                        deep_out.at[use, dz],
                        deep_in.at[use, dz],
                        sum_send.at[use, base + dz],
                        sum_recv.at[use, base + dz],
                        device,
                    )
                )
        for dz in range(1, leaves):
            third[dz - 1].wait_recv()
            mine = mine + deep_in[use, dz].astype(f32)
        return mine

    def spread(use, value):
        reduced[use, owner, block_rows(0), :] = value
        copies = {}
        for dz in range(1, leaves):
            here = reduced.at[use, owner, block_rows(0), :]
            copies[dz] = send(
                here, here, spread_send.at[use, dz], spread_recv.at[use, dz], level(dz)[1]
            )
        first, second = {}, []
        for dz in range(leaves):
            if dz:
                copies[dz].wait_recv()
            source = lax.rem(owner + leaves - dz, leaves)
            for i, d in enumerate(cross + [sib]):
                here = reduced.at[use, source, block_rows(0), :]
                slot = leaves * (i + 1) + dz
                first[d, dz] = send(
                    here, here, spread_send.at[use, slot], spread_recv.at[use, slot], peer(d)
                )
        base = leaves * (len(cross) + 2)
        for i, d in enumerate(cross):
            for dz in range(leaves):
                first[d, dz].wait_recv()
            here = reduced.at[use, :, block_rows(d), :]
            second.append(
                send(
                    here, here, spread_send.at[use, base + i], spread_recv.at[use, base + i], peer(sib)
                )
            )
        for dz in range(leaves):
            first[sib, dz].wait_recv()
        for copy in second:
            copy.wait_recv()

    def scale_leaf():
        for c in range(local // step):
            rows = pl.ds(c * step, step)
            joined = (
                doff[:, pl.ds(c * tile_rows, tile_rows)]
                * pairs[:, pl.ds(c * tile_rows, tile_rows)].astype(f32)
            )
            scaled = paired(
                forward[rows, :].astype(f32), column_of(dinv[:, rows], 1), column_of(joined, 2)
            )
            scaled_t[:, rows] = scaled.T

    gathered = sum_all(0, scale_leaf)
    spread(0, (root_rhs[...].astype(f32) - gathered).astype(bf16))
    root_load.wait()
    root_forward = jnp.zeros((root_inv.shape[0], root_rhs.shape[1]), f32)
    for z in range(leaves):
        root_forward = root_forward + jnp.dot(
            root_inv[:, z * band : (z + 1) * band], reduced[0, z], preferred_element_type=f32
        )
    root_scaled = paired(
        root_forward,
        column_of(root_dinv[...], 1),
        column_of(root_doff[...] * root_pairs[...].astype(f32), 2),
    )
    root_scaled_t = root_scaled.T.astype(bf16)
    for z in range(leaves):
        scattered[1, z] = jnp.dot(
            root_scaled_t, root_inv[:, z * band : (z + 1) * band], preferred_element_type=f32
        ).T
    root_own = sum_all(1, lambda: None).astype(bf16)
    out[pl.ds(local, own_rows), :] = root_own
    spread(1, root_own)

    for t in range(leaves * band_tiles):
        rows = pl.ds(t % band_tiles * tile_rows, tile_rows)
        whole_t[t] = reduced[1, t // band_tiles, rows, :].astype(f32).T
    for k in range(tile_count):
        values_t[:, k * tile_rows : (k + 1) * tile_rows] = whole_t[names[k]].astype(bf16)

    @pl.loop(0, local // step)
    def _(c):
        rows = pl.ds(pl.multiple_of(c * step, step), step)
        coupled = jnp.dot(values_t[...], update[:, rows], preferred_element_type=f32)
        vector_t[:, rows] = (scaled_t[:, rows] - coupled).astype(bf16)

    def back(d, target):
        @pl.loop(0, local // step)
        def _(c):
            rows = pl.ds(pl.multiple_of(c * step, step), step)
            target[:, rows] = jnp.dot(
                vector_t[...], inverse[d, :, rows], preferred_element_type=f32
            ).astype(target.dtype)

    first, later = {}, []
    lanes = halves

    def to_near(d):
        i = spots[d]
        back(d + sib, back_near_out.at[i])
        first[d] = send(
            back_near_out.at[i], back_near_in.at[i], back_send.at[i], back_recv.at[i], peer(sib)
        )

    def join(d):
        i = spots[d]
        first[d].wait_recv()
        back_keep[i] = back_keep[i] + back_near_in[i].astype(f32)

    def to_far(d, part, target, slot, device):
        i = spots[d]
        back_far_out[i, :, lanes[part]] = back_keep[i, :, lanes[part]].astype(bf16)
        return send(
            back_far_out.at[i, :, lanes[part]],
            target,
            back_send.at[slot],
            back_recv.at[slot],
            device,
        )

    base = len(spots)
    to_near(corner)
    back(corner, back_keep.at[spots[corner]])
    to_near(one)
    join(corner)
    relayed = [
        to_far(corner, 0, back_relay.at[0], base, peer(one)),
        to_far(corner, 1, back_relay.at[1], base + 1, peer(two)),
    ]
    back(one, back_keep.at[spots[one]])
    to_near(two)
    join(one)
    later.append(to_far(one, 0, back_far_in.at[0, :, lanes[0]], base + 2, peer(one)))
    back(two, back_keep.at[spots[two]])
    join(two)
    later.append(to_far(two, 1, back_far_in.at[1, :, lanes[1]], base + 3, peer(two)))
    for d, part, place in ((two, 0, 1), (one, 1, 0)):
        i = spots[d]
        relayed[part].wait_recv()
        back_keep[i, :, lanes[part]] = back_keep[i, :, lanes[part]] + back_relay[part].astype(f32)
        later.append(
            to_far(d, part, back_far_in.at[place, :, lanes[part]], base + 4 + part, peer(d))
        )
    to_near(0)
    back(0, back_keep.at[spots[0]])
    join(0)
    for copy in later:
        copy.wait_recv()
    result = back_keep[spots[0]] + back_far_in[0].astype(f32) + back_far_in[1].astype(f32)
    out[pl.ds(0, local), :] = result.T.astype(bf16)
    for copy in pending:
        copy.wait_send()


def in_one_kernel(
    leaf_rhs,
    leaf_inverse,
    leaf_update,
    root_tiles,
    leaf_dinv,
    leaf_doff,
    leaf_pairs,
    root_rhs,
    root_inverse,
    root_dinv,
    root_doff,
    root_pairs,
):
    f32, bf16 = jnp.float32, jnp.bfloat16
    leaves, tile_count = root_tiles.shape
    group_size = lax.axis_size("leaf") // leaves
    node_count = lax.axis_size("node")
    members = group_size * node_count
    local, rhs = leaf_rhs.shape[1:]
    own_rows, root_rows = root_inverse.shape
    band = members * own_rows
    padded = -(-own_rows // tile_rows) * tile_rows
    half = members // 2
    dma = pltpu.SemaphoreType.DMA
    hbm = pl.BlockSpec(memory_space=pl.ANY)
    vmem = pl.BlockSpec(memory_space=pltpu.VMEM)
    smem = pl.BlockSpec(memory_space=pltpu.SMEM)
    flops = 4 * rhs * (local * members * local + tile_count * tile_rows * local)
    both = pl.pallas_call(
        functools.partial(solve_kernel, leaves, group_size, node_count),
        out_shape=jax.ShapeDtypeStruct((local + own_rows, rhs), bf16),
        in_specs=[hbm, hbm, hbm, smem, vmem, vmem, vmem, vmem, hbm, vmem, vmem, vmem],
        out_specs=vmem,
        scratch_shapes=[
            pltpu.VMEM((members, local, rhs), bf16),
            pltpu.VMEM((members, local, local), bf16),
            pltpu.VMEM((tile_count * tile_rows, local), bf16),
            pltpu.VMEM((padded, root_rows), bf16),
            pltpu.VMEM((local, rhs), f32),
            pltpu.VMEM((local, rhs), bf16),
            pltpu.VMEM((tile_count, tile_rows, rhs), f32),
            pltpu.VMEM((rhs, local), f32),
            pltpu.VMEM((rhs, local), bf16),
            pltpu.VMEM((rhs, tile_count * tile_rows), bf16),
            pltpu.VMEM((root_rows // tile_rows, rhs, tile_rows), f32),
            pltpu.VMEM((2, leaves, band, rhs), f32),
            pltpu.VMEM((2, half, leaves, own_rows, rhs), bf16),
            pltpu.VMEM((2, half, leaves, own_rows, rhs), bf16),
            pltpu.VMEM((2, half, leaves, own_rows, rhs), bf16),
            pltpu.VMEM((2, half, leaves, own_rows, rhs), bf16),
            pltpu.VMEM((2, leaves, own_rows, rhs), bf16),
            pltpu.VMEM((2, leaves, own_rows, rhs), bf16),
            pltpu.VMEM((2, leaves, band, rhs), bf16),
            pltpu.VMEM((half, rhs, local), f32),
            pltpu.VMEM((half, rhs, local), bf16),
            pltpu.VMEM((half, rhs, local), bf16),
            pltpu.VMEM((half, rhs, local), bf16),
            pltpu.VMEM((2, rhs, local), bf16),
            pltpu.VMEM((2, rhs, local // 2), bf16),
            dma((members + 3,)),
            dma((members + 2,)),
            dma((members + 2,)),
            dma((2, leaves * (half + 2))),
            dma((2, leaves * (half + 2))),
            dma((2, leaves * (half + 2))),
            dma((2, leaves * (half + 2))),
            dma((members + 2,)),
            dma((members + 2,)),
        ],
        compiler_params=pltpu.CompilerParams(
            collective_id=0, has_side_effects=True, vmem_limit_bytes=56 * 2**20
        ),
        cost_estimate=pl.CostEstimate(
            flops=flops, bytes_accessed=2 * local * local * members, transcendentals=0
        ),
        name="solve",
    )(
        leaf_rhs,
        leaf_inverse,
        leaf_update,
        root_tiles,
        leaf_dinv,
        leaf_doff,
        leaf_pairs,
        root_rhs,
        root_inverse,
        root_dinv[None],
        root_doff[None],
        root_pairs[None],
    )
    return both[None, :local], both[local:]


def fits_kernel(leaf_rhs, root_tiles, root_rhs, group_size, node_count):
    members = group_size * node_count
    local, own_rows = leaf_rhs.shape[1], root_rhs.shape[0]
    return (
        group_size % 2 == 0
        and members == 8
        and 2 * members * local * local <= 20 * 2**20
        and leaf_rhs.shape[2] == tile_rows
        and local % (2 * tile_rows) == 0
        and own_rows % 16 == 0
        and members * own_rows % tile_rows == 0
    )


def by_shape(*arrays):
    leaf_rhs, root_tiles, root_rhs = arrays[0], arrays[3], arrays[7]
    group_size = lax.axis_size("leaf") // root_tiles.shape[0]
    if fits_kernel(leaf_rhs, root_tiles, root_rhs, group_size, lax.axis_size("node")):
        return in_one_kernel(*arrays)
    return on_device(*arrays)


def solution(mesh):
    in_specs = (
        P("leaf", "node", None),
        P("leaf", "node", None),
        P("leaf", None, "node"),
        P(),
        P("leaf", "node"),
        P("leaf", "node"),
        P("leaf", "node"),
        P(("leaf", "node"), None),
        P(("leaf", "node"), None),
        P(("leaf", "node")),
        P(("leaf", "node")),
        P(("leaf", "node")),
    )
    out_specs = (P("leaf", "node", None), P(("leaf", "node"), None))
    return jax.shard_map(
        by_shape, mesh=mesh, in_specs=in_specs, out_specs=out_specs, check_vma=False
    )
```

```python
import functools

import jax
import jax.numpy as jnp
from jax import lax
from jax.experimental import pallas as pl
from jax.experimental.pallas import tpu as pltpu
from jax.sharding import PartitionSpec as P

LEAVES = 4
ROOT_TILES = 24


tile_rows = 128


def partner(value, axis, apart):
    mask = 2**apart
    pairs = [(source, source ^ mask) for source in range(lax.axis_size(axis))]
    return lax.ppermute(value, axis, pairs)


def pivot_solve(values, diagonal, coupling, pairs):
    length = values.shape[0]
    halves = values.reshape(length // 2, 2, values.shape[1])
    diag_two = diagonal.reshape(length // 2, 2)
    joined = (coupling * pairs.astype(jnp.float32))[:, None]
    first_row = diag_two[:, 0:1] * halves[:, 0, :] + joined * halves[:, 1, :]
    second_row = joined * halves[:, 0, :] + diag_two[:, 1:2] * halves[:, 1, :]
    return jnp.stack([first_row, second_row], axis=1).reshape(length, values.shape[1])


def transposed_product(matrix, vector):
    return lax.dot_general(
        matrix, vector, (((0,), (0,)), ((), ())), preferred_element_type=jnp.float32
    )


def on_device(
    leaf_rhs,
    leaf_inverse,
    leaf_update,
    root_tiles,
    leaf_dinv,
    leaf_doff,
    leaf_pairs,
    root_rhs,
    root_inverse,
    root_dinv,
    root_doff,
    root_pairs,
):
    factor_rows = leaf_inverse[0]
    local_rows = factor_rows.shape[0]
    rhs_count = leaf_rhs.shape[2]
    root_local = root_rhs.shape[0]
    group_size = lax.axis_size("leaf") // LEAVES
    node_count = lax.axis_size("node")
    bit_count = group_size.bit_length() - 1
    leaf_index = lax.axis_index("leaf")
    group_member = leaf_index % group_size
    leaf_owner = leaf_index // group_size
    block_rows = node_count * local_rows
    holding = lax.all_gather(leaf_rhs[0], "node", axis=0, tiled=True)
    block_start = group_member * block_rows
    own_columns = lax.dynamic_slice_in_dim(factor_rows, block_start, block_rows, 1)
    product_sum = jnp.dot(own_columns, holding, preferred_element_type=jnp.float32)
    for bit_number in range(bit_count):
        partner_rows = partner(holding, "leaf", bit_number)
        span_rows = holding.shape[0]
        partner_start = (group_member >> bit_number ^ 1) * span_rows
        columns = lax.dynamic_slice_in_dim(factor_rows, partner_start, span_rows, 1)
        product_sum = product_sum + jnp.dot(
            columns, partner_rows, preferred_element_type=jnp.float32
        )
        if bit_number + 1 < bit_count:
            low_side = group_member >> bit_number & 1 == 0
            holding = jnp.where(
                low_side,
                jnp.concatenate([holding, partner_rows], 0),
                jnp.concatenate([partner_rows, holding], 0),
            )
    leaf_forward = product_sum.astype(jnp.bfloat16)
    update_rows = leaf_update[0]
    tile_ids = lax.dynamic_index_in_dim(root_tiles, leaf_owner, 0, keepdims=False)
    tile_count = tile_ids.shape[0]
    onehot = (jnp.arange(ROOT_TILES, dtype=jnp.int32)[:, None] == tile_ids[None, :]).astype(
        jnp.float32
    )
    update_term = jnp.dot(update_rows, leaf_forward, preferred_element_type=jnp.float32)
    scattered = jnp.einsum(
        "tk,kar->tar",
        onehot,
        update_term.reshape(tile_count, tile_rows, rhs_count),
        precision=lax.Precision.HIGHEST,
    )
    scattered = scattered.reshape(ROOT_TILES * tile_rows, rhs_count)
    offset = lax.axis_index(("leaf", "node")) * root_local
    own_rows = lax.dynamic_update_slice_in_dim(
        jnp.zeros_like(scattered), root_rhs.astype(jnp.float32), offset, 0
    )
    merged = lax.psum(own_rows - scattered, ("leaf", "node")).astype(jnp.bfloat16)
    root_forward = jnp.dot(root_inverse, merged, preferred_element_type=jnp.float32)
    root_scaled = pivot_solve(root_forward, root_dinv, root_doff, root_pairs).astype(jnp.bfloat16)
    full_term = transposed_product(root_inverse, root_scaled)
    root_full = lax.psum(full_term, ("leaf", "node")).astype(jnp.bfloat16)
    own_offset = lax.axis_index(("leaf", "node")) * root_local
    root_own = lax.dynamic_slice_in_dim(root_full, own_offset, root_local, 0)
    tile_values = jnp.einsum(
        "tk,tar->kar",
        onehot.astype(jnp.bfloat16),
        root_full.reshape(ROOT_TILES, tile_rows, rhs_count),
        preferred_element_type=jnp.float32,
    )
    tile_values = tile_values.astype(jnp.bfloat16).reshape(tile_count * tile_rows, rhs_count)
    coupling_term = transposed_product(update_rows, tile_values)
    leaf_scaled = pivot_solve(
        leaf_forward.astype(jnp.float32), leaf_dinv[0], leaf_doff[0], leaf_pairs[0]
    )
    leaf_vector = (leaf_scaled - coupling_term).astype(jnp.bfloat16)
    back_term = transposed_product(factor_rows, leaf_vector)
    for bit_number in reversed(range(bit_count)):
        half_rows = back_term.shape[0] // 2
        lower_rows = back_term[:half_rows]
        upper_rows = back_term[half_rows:]
        high_side = group_member >> bit_number & 1 == 1
        outgoing = jnp.where(high_side, lower_rows, upper_rows)
        keeping = jnp.where(high_side, upper_rows, lower_rows)
        back_term = keeping + partner(outgoing.astype(jnp.bfloat16), "leaf", bit_number).astype(
            outgoing.dtype
        )
    leaf_solution = lax.psum_scatter(
        back_term.astype(jnp.bfloat16), "node", scatter_dimension=0, tiled=True
    )
    return (leaf_solution[None], root_own)


def flipped(value, mask):
    bit = 1
    while bit <= mask:
        if mask & bit:
            value = value + bit - 2 * bit * lax.rem(lax.div(value, bit), 2)
        bit *= 2
    return value


def column_of(row, group):
    count = row.shape[1]
    length = -(-count * group // tile_rows) * tile_rows
    shape = (length, count)
    place = lax.broadcasted_iota(jnp.int32, shape, 0)
    if group > 1:
        place = lax.div(place, group)
    lane = lax.broadcasted_iota(jnp.int32, shape, 1)
    return jnp.sum(jnp.where(place == lane, row, 0.0), axis=1, keepdims=True)


def paired(values, diagonal, joined):
    length = values.shape[0]
    odd = lax.rem(lax.broadcasted_iota(jnp.int32, values.shape, 0), 2) == 1
    other = jnp.where(odd, pltpu.roll(values, 1, 0), pltpu.roll(values, length - 1, 0))
    return diagonal * values + joined * other


def solve_kernel(
    leaves,
    group_size,
    node_count,
    rhs_hbm,
    inverse_hbm,
    update_hbm,
    tiles,
    dinv,
    doff,
    pairs,
    root_rhs,
    root_inv_hbm,
    root_dinv,
    root_doff,
    root_pairs,
    out,
    right,
    inverse,
    update,
    root_inv,
    total,
    forward,
    term,
    scaled_t,
    vector_t,
    values_t,
    whole,
    scattered,
    near_out,
    near_in,
    far_out,
    far_in,
    deep_out,
    deep_in,
    reduced,
    back_keep,
    back_near_out,
    back_near_in,
    back_far_out,
    back_far_in,
    back_relay,
    load_sem,
    right_send,
    right_recv,
    sum_send,
    sum_recv,
    spread_send,
    spread_recv,
    back_send,
    back_recv,
):
    f32, bf16 = jnp.float32, jnp.bfloat16
    leaf = lax.axis_index("leaf")
    node = lax.axis_index("node")
    owner = lax.div(leaf, group_size)
    member = lax.rem(leaf, group_size) * node_count + node
    members = group_size * node_count
    sib = node_count
    cross = sorted((d for d in range(1, members) if not d & sib), key=lambda d: -bin(d).count("1"))
    local = rhs_hbm.shape[1]
    own_rows = root_rhs.shape[0]
    band = members * own_rows
    band_tiles = band // tile_rows
    step = 2 * tile_rows
    pending = []

    def peer(d):
        return flipped(leaf, d // node_count), flipped(node, d % node_count)

    def level(dz):
        other = lax.rem(owner + dz, leaves)
        return other, (lax.rem(leaf + dz * group_size, leaves * group_size), node)

    def send(source, target, send_sem, recv_sem, device):
        copy = pltpu.make_async_remote_copy(
            src_ref=source,
            dst_ref=target,
            send_sem=send_sem,
            recv_sem=recv_sem,
            device_id=device,
            device_id_type=pl.DeviceIdType.MESH,
        )
        copy.start()
        pending.append(copy)
        return copy

    corner, one, two = cross
    order = [0, sib, one, two, one + sib, two + sib, corner, corner + sib]
    loads = {}
    for d in order:
        start = pl.multiple_of(flipped(member, d) * local, tile_rows)
        loads[d] = pltpu.make_async_copy(
            inverse_hbm.at[0, :, pl.ds(start, local)], inverse.at[d], load_sem.at[d]
        )
    own_load = pltpu.make_async_copy(rhs_hbm.at[0], right.at[0], load_sem.at[members])
    update_load = pltpu.make_async_copy(update_hbm.at[0], update, load_sem.at[members + 1])
    root_load = pltpu.make_async_copy(
        root_inv_hbm, root_inv.at[pl.ds(0, own_rows)], load_sem.at[members + 2]
    )
    own_load.start()
    for d in order:
        loads[d].start()
    update_load.start()
    root_load.start()

    near = [sib] + cross
    barrier = pltpu.get_barrier_semaphore()
    for d in near:
        pl.semaphore_signal(
            barrier, inc=1, device_id=peer(d), device_id_type=pl.DeviceIdType.MESH
        )
    for dz in range(1, leaves):
        pl.semaphore_signal(
            barrier, inc=1, device_id=level(dz)[1], device_id_type=pl.DeviceIdType.MESH
        )
    pl.semaphore_wait(barrier, len(near) + leaves - 1)

    halves = [pl.ds(0, local // 2), pl.ds(local // 2, local // 2)]
    arrivals, late = {}, {}

    def own_half(d, rows, slot):
        return send(
            rhs_hbm.at[0, rows],
            right.at[d, rows],
            right_send.at[slot],
            right_recv.at[slot],
            peer(d),
        )

    arrivals[one] = own_half(one, halves[0], one)
    arrivals[two] = own_half(two, halves[1], two)
    arrivals[sib] = own_half(sib, pl.ds(0, local), sib)
    late[one] = own_half(one, halves[1], members + 2)
    late[two] = own_half(two, halves[0], members + 3)
    total[...] = jnp.zeros_like(total)
    if root_inv.shape[0] > own_rows:
        root_inv[own_rows:, :] = jnp.zeros(
            (root_inv.shape[0] - own_rows, root_inv.shape[1]), bf16
        )

    def product(d):
        loads[d].wait()

        @pl.loop(0, 2)
        def _(i):
            rows = pl.ds(pl.multiple_of(i * (local // 2), tile_rows), local // 2)
            total[rows, :] += jnp.dot(
                inverse[d, rows, :], right[d], preferred_element_type=f32
            )

    def to_sibling(d, rows, slot):
        return send(
            right.at[d, rows],
            right.at[d + sib, rows],
            right_send.at[slot],
            right_recv.at[slot],
            peer(sib),
        )

    own_load.wait()
    product(0)
    arrivals[sib].wait_recv()
    product(sib)
    corner_halves = []
    for d, other, rows, slot in ((one, two, halves[0], corner), (two, one, halves[1], members)):
        arrivals[d].wait_recv()
        corner_halves.append(
            send(
                right.at[d, rows],
                right.at[corner, rows],
                right_send.at[slot],
                right_recv.at[slot],
                peer(other),
            )
        )
    for d in (one, two):
        late[d].wait_recv()
        arrivals[d + sib] = to_sibling(d, pl.ds(0, local), d + sib)
    product(one)
    product(two)
    arrivals[one + sib].wait_recv()
    product(one + sib)
    last = []
    for copy, rows, slot in zip(corner_halves, halves, (corner + sib, members + 1)):
        copy.wait_recv()
        last.append(to_sibling(corner, rows, slot))
    arrivals[two + sib].wait_recv()
    product(two + sib)
    product(corner)
    for copy in last:
        copy.wait_recv()
    product(corner + sib)
    forward[...] = total[...].astype(bf16)

    update_load.wait()
    tile_count = update.shape[0] // tile_rows

    batch = 4 if tile_count % 4 == 0 else 1

    @pl.loop(0, tile_count // batch)
    def _(k):
        length = batch * tile_rows
        rows = pl.ds(pl.multiple_of(k * length, length), length)
        product_rows = jnp.dot(update[rows, :], forward[...], preferred_element_type=f32)
        term[pl.ds(k * batch, batch)] = product_rows.reshape(batch, *term.shape[1:])

    names = [tiles[owner, k] for k in range(tile_count)]
    for t in range(leaves * band_tiles):
        rows = pl.ds(t % band_tiles * tile_rows, tile_rows)
        placed = jnp.zeros(term.shape[1:], f32)
        for k in range(tile_count):
            placed = jnp.where(names[k] == t, term[k], placed)
        scattered[0, t // band_tiles, rows, :] = placed

    def block_rows(d):
        return pl.ds(pl.multiple_of(flipped(member, d) * own_rows, 16), own_rows)

    spots = {d: i for i, d in enumerate(cross + [0])}

    def sum_all(use, meanwhile):
        first, second = {}, {}
        for d in cross + [0]:
            i = spots[d]
            near_out[use, i] = scattered[use, :, block_rows(d + sib), :].astype(bf16)
            first[d] = send(
                near_out.at[use, i],
                near_in.at[use, i],
                sum_send.at[use, i],
                sum_recv.at[use, i],
                peer(sib),
            )
        base = len(spots)
        turns = list(range(1, leaves)) + [0]
        for d in cross:
            i = spots[d]
            first[d].wait_recv()
            both = scattered[use, :, block_rows(d), :] + near_in[use, i].astype(f32)
            far_out[use, i] = both.astype(bf16)
            for dz in turns:
                other = level(dz)[0]
                slot = base + i * leaves + dz
                second[d, dz] = send(
                    far_out.at[use, i, other],
                    far_in.at[use, i, other],
                    sum_send.at[use, slot],
                    sum_recv.at[use, slot],
                    peer(d),
                )
        meanwhile()
        first[0].wait_recv()
        base += len(cross) * leaves
        third = []
        for dz in turns:
            other, device = level(dz)
            mine = scattered[use, other, block_rows(0), :]
            mine = mine + near_in[use, spots[0], other].astype(f32)
            for d in cross:
                second[d, dz].wait_recv()
                mine = mine + far_in[use, spots[d], other].astype(f32)
            if dz:
                deep_out[use, dz] = mine.astype(bf16)
                third.append(
                    send(
                        deep_out.at[use, dz],
                        deep_in.at[use, dz],
                        sum_send.at[use, base + dz],
                        sum_recv.at[use, base + dz],
                        device,
                    )
                )
        for dz in range(1, leaves):
            third[dz - 1].wait_recv()
            mine = mine + deep_in[use, dz].astype(f32)
        return mine

    def spread(use, value):
        reduced[use, owner, block_rows(0), :] = value
        copies = {}
        for dz in range(1, leaves):
            here = reduced.at[use, owner, block_rows(0), :]
            copies[dz] = send(
                here, here, spread_send.at[use, dz], spread_recv.at[use, dz], level(dz)[1]
            )
        first, second = {}, []
        for dz in range(leaves):
            if dz:
                copies[dz].wait_recv()
            source = lax.rem(owner + leaves - dz, leaves)
            for i, d in enumerate(cross + [sib]):
                here = reduced.at[use, source, block_rows(0), :]
                slot = leaves * (i + 1) + dz
                first[d, dz] = send(
                    here, here, spread_send.at[use, slot], spread_recv.at[use, slot], peer(d)
                )
        base = leaves * (len(cross) + 2)
        for i, d in enumerate(cross):
            for dz in range(leaves):
                first[d, dz].wait_recv()
            here = reduced.at[use, :, block_rows(d), :]
            second.append(
                send(
                    here, here, spread_send.at[use, base + i], spread_recv.at[use, base + i], peer(sib)
                )
            )
        for dz in range(leaves):
            first[sib, dz].wait_recv()
        for copy in second:
            copy.wait_recv()

    def scale_leaf():
        for c in range(local // step):
            rows = pl.ds(c * step, step)
            joined = (
                doff[:, pl.ds(c * tile_rows, tile_rows)]
                * pairs[:, pl.ds(c * tile_rows, tile_rows)].astype(f32)
            )
            scaled = paired(
                forward[rows, :].astype(f32), column_of(dinv[:, rows], 1), column_of(joined, 2)
            )
            scaled_t[:, rows] = scaled.T
        columns.append(column_of(root_dinv[...], 1))
        columns.append(column_of(root_doff[...] * root_pairs[...].astype(f32), 2))

    columns = []
    gathered = sum_all(0, scale_leaf)
    spread(0, (root_rhs[...].astype(f32) - gathered).astype(bf16))
    root_load.wait()
    root_forward = jnp.zeros((root_inv.shape[0], root_rhs.shape[1]), f32)
    for z in range(leaves):
        root_forward = root_forward + jnp.dot(
            root_inv[:, z * band : (z + 1) * band], reduced[0, z], preferred_element_type=f32
        )
    root_scaled = paired(root_forward, *columns)
    root_scaled_t = root_scaled.T.astype(bf16)
    for z in range(leaves):
        scattered[1, z] = jnp.dot(
            root_scaled_t, root_inv[:, z * band : (z + 1) * band], preferred_element_type=f32
        ).T
    root_own = sum_all(1, lambda: None).astype(bf16)
    out[pl.ds(local, own_rows), :] = root_own
    spread(1, root_own)

    for t in range(leaves * band_tiles):
        rows = pl.ds(t % band_tiles * tile_rows, tile_rows)
        whole[t] = reduced[1, t // band_tiles, rows, :].astype(f32)
    for k in range(tile_count):
        values_t[:, k * tile_rows : (k + 1) * tile_rows] = whole[names[k]].T.astype(bf16)

    @pl.loop(0, local // step)
    def _(c):
        rows = pl.ds(pl.multiple_of(c * step, step), step)
        coupled = jnp.dot(values_t[...], update[:, rows], preferred_element_type=f32)
        vector_t[:, rows] = (scaled_t[:, rows] - coupled).astype(bf16)

    def back(d, target, part=None):
        steps = local // step
        start, stop = (0, steps) if part is None else (part * steps // 2, (part + 1) * steps // 2)

        @pl.loop(start, stop)
        def _(c):
            rows = pl.ds(pl.multiple_of(c * step, step), step)
            target[:, rows] = jnp.dot(
                vector_t[...], inverse[d, :, rows], preferred_element_type=f32
            ).astype(target.dtype)

    first, later = {}, []
    lanes = halves

    def to_near(d):
        i = spots[d]
        back(d + sib, back_near_out.at[i])
        first[d] = send(
            back_near_out.at[i], back_near_in.at[i], back_send.at[i], back_recv.at[i], peer(sib)
        )

    def join(d):
        i = spots[d]
        first[d].wait_recv()
        back_keep[i] = back_keep[i] + back_near_in[i].astype(f32)

    def to_far(d, part, target, slot, device):
        i = spots[d]
        back_far_out[i, :, lanes[part]] = back_keep[i, :, lanes[part]].astype(bf16)
        return send(
            back_far_out.at[i, :, lanes[part]],
            target,
            back_send.at[slot],
            back_recv.at[slot],
            device,
        )

    base = len(spots)
    i = spots[corner]
    corner_near, relayed = [], []

    def corner_near_half(part):
        back(corner + sib, back_near_out.at[i], part)
        slot = i if part == 0 else base + 6
        corner_near.append(
            send(
                back_near_out.at[i, :, lanes[part]],
                back_near_in.at[i, :, lanes[part]],
                back_send.at[slot],
                back_recv.at[slot],
                peer(sib),
            )
        )

    def corner_far_half(part, device):
        corner_near[part].wait_recv()
        back_keep[i, :, lanes[part]] = back_keep[i, :, lanes[part]] + back_near_in[
            i, :, lanes[part]
        ].astype(f32)
        relayed.append(to_far(corner, part, back_relay.at[part], base + part, device))

    corner_near_half(0)
    back(corner, back_keep.at[i], 0)
    corner_near_half(1)
    corner_far_half(0, peer(one))
    back(corner, back_keep.at[i], 1)
    to_near(one)
    corner_far_half(1, peer(two))
    back(one, back_keep.at[spots[one]])
    to_near(two)
    join(one)
    later.append(to_far(one, 0, back_far_in.at[0, :, lanes[0]], base + 2, peer(one)))
    back(two, back_keep.at[spots[two]])
    join(two)
    later.append(to_far(two, 1, back_far_in.at[1, :, lanes[1]], base + 3, peer(two)))
    for d, part, place in ((two, 0, 1), (one, 1, 0)):
        i = spots[d]
        relayed[part].wait_recv()
        back_keep[i, :, lanes[part]] = back_keep[i, :, lanes[part]] + back_relay[part].astype(f32)
        later.append(
            to_far(d, part, back_far_in.at[place, :, lanes[part]], base + 4 + part, peer(d))
        )
    to_near(0)
    back(0, back_keep.at[spots[0]])
    join(0)
    for copy in later:
        copy.wait_recv()
    result = back_keep[spots[0]] + back_far_in[0].astype(f32) + back_far_in[1].astype(f32)
    out[pl.ds(0, local), :] = result.T.astype(bf16)
    for copy in pending:
        copy.wait_send()


def in_one_kernel(
    leaf_rhs,
    leaf_inverse,
    leaf_update,
    root_tiles,
    leaf_dinv,
    leaf_doff,
    leaf_pairs,
    root_rhs,
    root_inverse,
    root_dinv,
    root_doff,
    root_pairs,
):
    f32, bf16 = jnp.float32, jnp.bfloat16
    leaves, tile_count = root_tiles.shape
    group_size = lax.axis_size("leaf") // leaves
    node_count = lax.axis_size("node")
    members = group_size * node_count
    local, rhs = leaf_rhs.shape[1:]
    own_rows, root_rows = root_inverse.shape
    band = members * own_rows
    padded = -(-own_rows // tile_rows) * tile_rows
    half = members // 2
    dma = pltpu.SemaphoreType.DMA
    hbm = pl.BlockSpec(memory_space=pl.ANY)
    vmem = pl.BlockSpec(memory_space=pltpu.VMEM)
    smem = pl.BlockSpec(memory_space=pltpu.SMEM)
    flops = 4 * rhs * (local * members * local + tile_count * tile_rows * local)
    both = pl.pallas_call(
        functools.partial(solve_kernel, leaves, group_size, node_count),
        out_shape=jax.ShapeDtypeStruct((local + own_rows, rhs), bf16),
        in_specs=[hbm, hbm, hbm, smem, vmem, vmem, vmem, vmem, hbm, vmem, vmem, vmem],
        out_specs=vmem,
        scratch_shapes=[
            pltpu.VMEM((members, local, rhs), bf16),
            pltpu.VMEM((members, local, local), bf16),
            pltpu.VMEM((tile_count * tile_rows, local), bf16),
            pltpu.VMEM((padded, root_rows), bf16),
            pltpu.VMEM((local, rhs), f32),
            pltpu.VMEM((local, rhs), bf16),
            pltpu.VMEM((tile_count, tile_rows, rhs), f32),
            pltpu.VMEM((rhs, local), f32),
            pltpu.VMEM((rhs, local), bf16),
            pltpu.VMEM((rhs, tile_count * tile_rows), bf16),
            pltpu.VMEM((root_rows // tile_rows, rhs, tile_rows), f32),
            pltpu.VMEM((2, leaves, band, rhs), f32),
            pltpu.VMEM((2, half, leaves, own_rows, rhs), bf16),
            pltpu.VMEM((2, half, leaves, own_rows, rhs), bf16),
            pltpu.VMEM((2, half, leaves, own_rows, rhs), bf16),
            pltpu.VMEM((2, half, leaves, own_rows, rhs), bf16),
            pltpu.VMEM((2, leaves, own_rows, rhs), bf16),
            pltpu.VMEM((2, leaves, own_rows, rhs), bf16),
            pltpu.VMEM((2, leaves, band, rhs), bf16),
            pltpu.VMEM((half, rhs, local), f32),
            pltpu.VMEM((half, rhs, local), bf16),
            pltpu.VMEM((half, rhs, local), bf16),
            pltpu.VMEM((half, rhs, local), bf16),
            pltpu.VMEM((2, rhs, local), bf16),
            pltpu.VMEM((2, rhs, local // 2), bf16),
            dma((members + 3,)),
            dma((members + 4,)),
            dma((members + 4,)),
            dma((2, leaves * (half + 2))),
            dma((2, leaves * (half + 2))),
            dma((2, leaves * (half + 2))),
            dma((2, leaves * (half + 2))),
            dma((members + 3,)),
            dma((members + 3,)),
        ],
        compiler_params=pltpu.CompilerParams(
            collective_id=0, has_side_effects=True, vmem_limit_bytes=56 * 2**20
        ),
        cost_estimate=pl.CostEstimate(
            flops=flops, bytes_accessed=2 * local * local * members, transcendentals=0
        ),
        name="solve",
    )(
        leaf_rhs,
        leaf_inverse,
        leaf_update,
        root_tiles,
        leaf_dinv,
        leaf_doff,
        leaf_pairs,
        root_rhs,
        root_inverse,
        root_dinv[None],
        root_doff[None],
        root_pairs[None],
    )
    return both[None, :local], both[local:]


def fits_kernel(leaf_rhs, root_tiles, root_rhs, group_size, node_count):
    members = group_size * node_count
    local, own_rows = leaf_rhs.shape[1], root_rhs.shape[0]
    return (
        group_size % 2 == 0
        and members == 8
        and 2 * members * local * local <= 20 * 2**20
        and leaf_rhs.shape[2] == tile_rows
        and local % (2 * tile_rows) == 0
        and own_rows % 16 == 0
        and members * own_rows % tile_rows == 0
    )


def by_shape(*arrays):
    leaf_rhs, root_tiles, root_rhs = arrays[0], arrays[3], arrays[7]
    group_size = lax.axis_size("leaf") // root_tiles.shape[0]
    if fits_kernel(leaf_rhs, root_tiles, root_rhs, group_size, lax.axis_size("node")):
        return in_one_kernel(*arrays)
    return on_device(*arrays)


def solution(mesh):
    in_specs = (
        P("leaf", "node", None),
        P("leaf", "node", None),
        P("leaf", None, "node"),
        P(),
        P("leaf", "node"),
        P("leaf", "node"),
        P("leaf", "node"),
        P(("leaf", "node"), None),
        P(("leaf", "node"), None),
        P(("leaf", "node")),
        P(("leaf", "node")),
        P(("leaf", "node")),
    )
    out_specs = (P("leaf", "node", None), P(("leaf", "node"), None))
    return jax.shard_map(
        by_shape, mesh=mesh, in_specs=in_specs, out_specs=out_specs, check_vma=False
    )
```

```python
import functools

import jax
import jax.numpy as jnp
from jax import lax
from jax.experimental import pallas as pl
from jax.experimental.pallas import tpu as pltpu
from jax.sharding import PartitionSpec as P

LEAVES = 4
ROOT_TILES = 24


tile_rows = 128


def partner(value, axis, apart):
    mask = 2**apart
    pairs = [(source, source ^ mask) for source in range(lax.axis_size(axis))]
    return lax.ppermute(value, axis, pairs)


def pivot_solve(values, diagonal, coupling, pairs):
    length = values.shape[0]
    halves = values.reshape(length // 2, 2, values.shape[1])
    diag_two = diagonal.reshape(length // 2, 2)
    joined = (coupling * pairs.astype(jnp.float32))[:, None]
    first_row = diag_two[:, 0:1] * halves[:, 0, :] + joined * halves[:, 1, :]
    second_row = joined * halves[:, 0, :] + diag_two[:, 1:2] * halves[:, 1, :]
    return jnp.stack([first_row, second_row], axis=1).reshape(length, values.shape[1])


def transposed_product(matrix, vector):
    return lax.dot_general(
        matrix, vector, (((0,), (0,)), ((), ())), preferred_element_type=jnp.float32
    )


def on_device(
    leaf_rhs,
    leaf_inverse,
    leaf_update,
    root_tiles,
    leaf_dinv,
    leaf_doff,
    leaf_pairs,
    root_rhs,
    root_inverse,
    root_dinv,
    root_doff,
    root_pairs,
):
    factor_rows = leaf_inverse[0]
    local_rows = factor_rows.shape[0]
    rhs_count = leaf_rhs.shape[2]
    root_local = root_rhs.shape[0]
    group_size = lax.axis_size("leaf") // LEAVES
    node_count = lax.axis_size("node")
    bit_count = group_size.bit_length() - 1
    leaf_index = lax.axis_index("leaf")
    group_member = leaf_index % group_size
    leaf_owner = leaf_index // group_size
    block_rows = node_count * local_rows
    holding = lax.all_gather(leaf_rhs[0], "node", axis=0, tiled=True)
    block_start = group_member * block_rows
    own_columns = lax.dynamic_slice_in_dim(factor_rows, block_start, block_rows, 1)
    product_sum = jnp.dot(own_columns, holding, preferred_element_type=jnp.float32)
    for bit_number in range(bit_count):
        partner_rows = partner(holding, "leaf", bit_number)
        span_rows = holding.shape[0]
        partner_start = (group_member >> bit_number ^ 1) * span_rows
        columns = lax.dynamic_slice_in_dim(factor_rows, partner_start, span_rows, 1)
        product_sum = product_sum + jnp.dot(
            columns, partner_rows, preferred_element_type=jnp.float32
        )
        if bit_number + 1 < bit_count:
            low_side = group_member >> bit_number & 1 == 0
            holding = jnp.where(
                low_side,
                jnp.concatenate([holding, partner_rows], 0),
                jnp.concatenate([partner_rows, holding], 0),
            )
    leaf_forward = product_sum.astype(jnp.bfloat16)
    update_rows = leaf_update[0]
    tile_ids = lax.dynamic_index_in_dim(root_tiles, leaf_owner, 0, keepdims=False)
    tile_count = tile_ids.shape[0]
    onehot = (jnp.arange(ROOT_TILES, dtype=jnp.int32)[:, None] == tile_ids[None, :]).astype(
        jnp.float32
    )
    update_term = jnp.dot(update_rows, leaf_forward, preferred_element_type=jnp.float32)
    scattered = jnp.einsum(
        "tk,kar->tar",
        onehot,
        update_term.reshape(tile_count, tile_rows, rhs_count),
        precision=lax.Precision.HIGHEST,
    )
    scattered = scattered.reshape(ROOT_TILES * tile_rows, rhs_count)
    offset = lax.axis_index(("leaf", "node")) * root_local
    own_rows = lax.dynamic_update_slice_in_dim(
        jnp.zeros_like(scattered), root_rhs.astype(jnp.float32), offset, 0
    )
    merged = lax.psum(own_rows - scattered, ("leaf", "node")).astype(jnp.bfloat16)
    root_forward = jnp.dot(root_inverse, merged, preferred_element_type=jnp.float32)
    root_scaled = pivot_solve(root_forward, root_dinv, root_doff, root_pairs).astype(jnp.bfloat16)
    full_term = transposed_product(root_inverse, root_scaled)
    root_full = lax.psum(full_term, ("leaf", "node")).astype(jnp.bfloat16)
    own_offset = lax.axis_index(("leaf", "node")) * root_local
    root_own = lax.dynamic_slice_in_dim(root_full, own_offset, root_local, 0)
    tile_values = jnp.einsum(
        "tk,tar->kar",
        onehot.astype(jnp.bfloat16),
        root_full.reshape(ROOT_TILES, tile_rows, rhs_count),
        preferred_element_type=jnp.float32,
    )
    tile_values = tile_values.astype(jnp.bfloat16).reshape(tile_count * tile_rows, rhs_count)
    coupling_term = transposed_product(update_rows, tile_values)
    leaf_scaled = pivot_solve(
        leaf_forward.astype(jnp.float32), leaf_dinv[0], leaf_doff[0], leaf_pairs[0]
    )
    leaf_vector = (leaf_scaled - coupling_term).astype(jnp.bfloat16)
    back_term = transposed_product(factor_rows, leaf_vector)
    for bit_number in reversed(range(bit_count)):
        half_rows = back_term.shape[0] // 2
        lower_rows = back_term[:half_rows]
        upper_rows = back_term[half_rows:]
        high_side = group_member >> bit_number & 1 == 1
        outgoing = jnp.where(high_side, lower_rows, upper_rows)
        keeping = jnp.where(high_side, upper_rows, lower_rows)
        back_term = keeping + partner(outgoing.astype(jnp.bfloat16), "leaf", bit_number).astype(
            outgoing.dtype
        )
    leaf_solution = lax.psum_scatter(
        back_term.astype(jnp.bfloat16), "node", scatter_dimension=0, tiled=True
    )
    return (leaf_solution[None], root_own)


def flipped(value, mask):
    bit = 1
    while bit <= mask:
        if mask & bit:
            value = value + bit - 2 * bit * lax.rem(lax.div(value, bit), 2)
        bit *= 2
    return value


def column_of(row, group):
    count = row.shape[1]
    length = -(-count * group // tile_rows) * tile_rows
    shape = (length, count)
    place = lax.broadcasted_iota(jnp.int32, shape, 0)
    if group > 1:
        place = lax.div(place, group)
    lane = lax.broadcasted_iota(jnp.int32, shape, 1)
    return jnp.sum(jnp.where(place == lane, row, 0.0), axis=1, keepdims=True)


def paired(values, diagonal, joined):
    length = values.shape[0]
    odd = lax.rem(lax.broadcasted_iota(jnp.int32, values.shape, 0), 2) == 1
    other = jnp.where(odd, pltpu.roll(values, 1, 0), pltpu.roll(values, length - 1, 0))
    return diagonal * values + joined * other


def solve_kernel(
    leaves,
    group_size,
    node_count,
    rhs_hbm,
    inverse_hbm,
    update_hbm,
    tiles,
    dinv,
    doff,
    pairs,
    root_rhs,
    root_inv_hbm,
    root_dinv,
    root_doff,
    root_pairs,
    out,
    right,
    inverse,
    update,
    root_inv,
    total,
    forward,
    term,
    scaled_t,
    vector_t,
    values_t,
    whole,
    scattered,
    near_out,
    near_in,
    far_out,
    far_in,
    deep_out,
    deep_in,
    reduced,
    back_keep,
    back_near_out,
    back_near_in,
    back_far_out,
    back_far_in,
    back_relay,
    load_sem,
    right_send,
    right_recv,
    sum_send,
    sum_recv,
    spread_send,
    spread_recv,
    back_send,
    back_recv,
):
    f32, bf16 = jnp.float32, jnp.bfloat16
    leaf = lax.axis_index("leaf")
    node = lax.axis_index("node")
    owner = lax.div(leaf, group_size)
    member = lax.rem(leaf, group_size) * node_count + node
    members = group_size * node_count
    sib = node_count
    cross = sorted((d for d in range(1, members) if not d & sib), key=lambda d: -bin(d).count("1"))
    local = rhs_hbm.shape[1]
    own_rows = root_rhs.shape[0]
    band = members * own_rows
    band_tiles = band // tile_rows
    step = 2 * tile_rows
    pending = []

    def peer(d):
        return flipped(leaf, d // node_count), flipped(node, d % node_count)

    def level(dz):
        other = lax.rem(owner + dz, leaves)
        return other, (lax.rem(leaf + dz * group_size, leaves * group_size), node)

    def send(source, target, send_sem, recv_sem, device):
        copy = pltpu.make_async_remote_copy(
            src_ref=source,
            dst_ref=target,
            send_sem=send_sem,
            recv_sem=recv_sem,
            device_id=device,
            device_id_type=pl.DeviceIdType.MESH,
        )
        copy.start()
        pending.append(copy)
        return copy

    corner, one, two = cross
    order = [0, sib, one, two, one + sib, two + sib, corner, corner + sib]
    loads = {}
    for d in order:
        start = pl.multiple_of(flipped(member, d) * local, tile_rows)
        loads[d] = pltpu.make_async_copy(
            inverse_hbm.at[0, :, pl.ds(start, local)], inverse.at[d], load_sem.at[d]
        )
    own_load = pltpu.make_async_copy(rhs_hbm.at[0], right.at[0], load_sem.at[members])
    update_load = pltpu.make_async_copy(update_hbm.at[0], update, load_sem.at[members + 1])
    root_load = pltpu.make_async_copy(
        root_inv_hbm, root_inv.at[pl.ds(0, own_rows)], load_sem.at[members + 2]
    )
    own_load.start()
    for d in order:
        loads[d].start()
    update_load.start()
    root_load.start()

    near = [sib] + cross
    barrier = pltpu.get_barrier_semaphore()
    for d in near:
        pl.semaphore_signal(
            barrier, inc=1, device_id=peer(d), device_id_type=pl.DeviceIdType.MESH
        )
    for dz in range(1, leaves):
        pl.semaphore_signal(
            barrier, inc=1, device_id=level(dz)[1], device_id_type=pl.DeviceIdType.MESH
        )
    pl.semaphore_wait(barrier, len(near) + leaves - 1)

    halves = [pl.ds(0, local // 2), pl.ds(local // 2, local // 2)]
    arrivals, late = {}, {}

    def own_half(d, rows, slot):
        return send(
            rhs_hbm.at[0, rows],
            right.at[d, rows],
            right_send.at[slot],
            right_recv.at[slot],
            peer(d),
        )

    arrivals[one] = own_half(one, halves[0], one)
    arrivals[two] = own_half(two, halves[1], two)
    arrivals[sib] = own_half(sib, pl.ds(0, local), sib)
    late[one] = own_half(one, halves[1], members + 2)
    late[two] = own_half(two, halves[0], members + 3)
    total[...] = jnp.zeros_like(total)
    if root_inv.shape[0] > own_rows:
        root_inv[own_rows:, :] = jnp.zeros(
            (root_inv.shape[0] - own_rows, root_inv.shape[1]), bf16
        )

    def product(d):
        loads[d].wait()

        total[...] += jnp.dot(inverse[d], right[d], preferred_element_type=f32)

    def to_sibling(d, rows, slot):
        return send(
            right.at[d, rows],
            right.at[d + sib, rows],
            right_send.at[slot],
            right_recv.at[slot],
            peer(sib),
        )

    own_load.wait()
    product(0)
    arrivals[sib].wait_recv()
    product(sib)
    corner_halves = []
    for d, other, rows, slot in ((one, two, halves[0], corner), (two, one, halves[1], members)):
        arrivals[d].wait_recv()
        corner_halves.append(
            send(
                right.at[d, rows],
                right.at[corner, rows],
                right_send.at[slot],
                right_recv.at[slot],
                peer(other),
            )
        )
    for d in (one, two):
        late[d].wait_recv()
        arrivals[d + sib] = to_sibling(d, pl.ds(0, local), d + sib)
    product(one)
    product(two)
    arrivals[one + sib].wait_recv()
    product(one + sib)
    last = []
    for copy, rows, slot in zip(corner_halves, halves, (corner + sib, members + 1)):
        copy.wait_recv()
        last.append(to_sibling(corner, rows, slot))
    arrivals[two + sib].wait_recv()
    product(two + sib)
    product(corner)
    for copy in last:
        copy.wait_recv()
    product(corner + sib)
    forward[...] = total[...].astype(bf16)

    update_load.wait()
    tile_count = update.shape[0] // tile_rows

    batch = tile_count // 2 if tile_count % 2 == 0 else 1

    @pl.loop(0, tile_count // batch)
    def _(k):
        length = batch * tile_rows
        rows = pl.ds(pl.multiple_of(k * length, length), length)
        product_rows = jnp.dot(update[rows, :], forward[...], preferred_element_type=f32)
        term[pl.ds(k * batch, batch)] = product_rows.reshape(batch, *term.shape[1:])

    names = [tiles[owner, k] for k in range(tile_count)]
    for t in range(leaves * band_tiles):
        rows = pl.ds(t % band_tiles * tile_rows, tile_rows)
        placed = jnp.zeros(term.shape[1:], f32)
        for k in range(tile_count):
            placed = jnp.where(names[k] == t, term[k], placed)
        scattered[0, t // band_tiles, rows, :] = placed

    def block_rows(d):
        return pl.ds(pl.multiple_of(flipped(member, d) * own_rows, 16), own_rows)

    spots = {d: i for i, d in enumerate(cross + [0])}

    def sum_all(use, meanwhile):
        first, second = {}, {}
        for d in cross + [0]:
            i = spots[d]
            near_out[use, i] = scattered[use, :, block_rows(d + sib), :].astype(bf16)
            first[d] = send(
                near_out.at[use, i],
                near_in.at[use, i],
                sum_send.at[use, i],
                sum_recv.at[use, i],
                peer(sib),
            )
        base = len(spots)
        turns = list(range(1, leaves)) + [0]
        for d in cross:
            i = spots[d]
            first[d].wait_recv()
            both = scattered[use, :, block_rows(d), :] + near_in[use, i].astype(f32)
            far_out[use, i] = both.astype(bf16)
            for dz in turns:
                other = level(dz)[0]
                slot = base + i * leaves + dz
                second[d, dz] = send(
                    far_out.at[use, i, other],
                    far_in.at[use, i, other],
                    sum_send.at[use, slot],
                    sum_recv.at[use, slot],
                    peer(d),
                )
        meanwhile()
        first[0].wait_recv()
        base += len(cross) * leaves
        third = []
        for dz in turns:
            other, device = level(dz)
            mine = scattered[use, other, block_rows(0), :]
            mine = mine + near_in[use, spots[0], other].astype(f32)
            for d in cross:
                second[d, dz].wait_recv()
                mine = mine + far_in[use, spots[d], other].astype(f32)
            if dz:
                deep_out[use, dz] = mine.astype(bf16)
                third.append(
                    send(
                        deep_out.at[use, dz],
                        deep_in.at[use, dz],
                        sum_send.at[use, base + dz],
                        sum_recv.at[use, base + dz],
                        device,
                    )
                )
        for dz in range(1, leaves):
            third[dz - 1].wait_recv()
            mine = mine + deep_in[use, dz].astype(f32)
        return mine

    def spread(use, value):
        reduced[use, owner, block_rows(0), :] = value
        copies = {}
        for dz in range(1, leaves):
            here = reduced.at[use, owner, block_rows(0), :]
            copies[dz] = send(
                here, here, spread_send.at[use, dz], spread_recv.at[use, dz], level(dz)[1]
            )
        first, second = {}, []
        for dz in range(leaves):
            if dz:
                copies[dz].wait_recv()
            source = lax.rem(owner + leaves - dz, leaves)
            for i, d in enumerate(cross + [sib]):
                here = reduced.at[use, source, block_rows(0), :]
                slot = leaves * (i + 1) + dz
                first[d, dz] = send(
                    here, here, spread_send.at[use, slot], spread_recv.at[use, slot], peer(d)
                )
        base = leaves * (len(cross) + 2)
        for i, d in enumerate(cross):
            for dz in range(leaves):
                first[d, dz].wait_recv()
            here = reduced.at[use, :, block_rows(d), :]
            second.append(
                send(
                    here, here, spread_send.at[use, base + i], spread_recv.at[use, base + i], peer(sib)
                )
            )
        for dz in range(leaves):
            first[sib, dz].wait_recv()
        for copy in second:
            copy.wait_recv()

    def scale_leaf():
        for c in range(local // step):
            rows = pl.ds(c * step, step)
            joined = (
                doff[:, pl.ds(c * tile_rows, tile_rows)]
                * pairs[:, pl.ds(c * tile_rows, tile_rows)].astype(f32)
            )
            scaled = paired(
                forward[rows, :].astype(f32), column_of(dinv[:, rows], 1), column_of(joined, 2)
            )
            scaled_t[:, rows] = scaled.T
        columns.append(column_of(root_dinv[...], 1))
        columns.append(column_of(root_doff[...] * root_pairs[...].astype(f32), 2))

    columns = []
    gathered = sum_all(0, scale_leaf)
    spread(0, (root_rhs[...].astype(f32) - gathered).astype(bf16))
    root_load.wait()
    root_forward = jnp.zeros((root_inv.shape[0], root_rhs.shape[1]), f32)
    for z in range(leaves):
        root_forward = root_forward + jnp.dot(
            root_inv[:, z * band : (z + 1) * band], reduced[0, z], preferred_element_type=f32
        )
    root_scaled = paired(root_forward, *columns)
    root_scaled_t = root_scaled.T.astype(bf16)
    for z in range(leaves):
        scattered[1, z] = jnp.dot(
            root_scaled_t, root_inv[:, z * band : (z + 1) * band], preferred_element_type=f32
        ).T
    root_own = sum_all(1, lambda: None).astype(bf16)
    out[pl.ds(local, own_rows), :] = root_own
    spread(1, root_own)

    for t in range(leaves * band_tiles):
        rows = pl.ds(t % band_tiles * tile_rows, tile_rows)
        whole[t] = reduced[1, t // band_tiles, rows, :].astype(f32)
    for k in range(tile_count):
        values_t[:, k * tile_rows : (k + 1) * tile_rows] = whole[names[k]].T.astype(bf16)

    @pl.loop(0, local // step)
    def _(c):
        rows = pl.ds(pl.multiple_of(c * step, step), step)
        coupled = jnp.dot(values_t[...], update[:, rows], preferred_element_type=f32)
        vector_t[:, rows] = (scaled_t[:, rows] - coupled).astype(bf16)

    def back(d, target, part=None):
        steps = local // step
        start, stop = (0, steps) if part is None else (part * steps // 2, (part + 1) * steps // 2)

        @pl.loop(start, stop)
        def _(c):
            rows = pl.ds(pl.multiple_of(c * step, step), step)
            target[:, rows] = jnp.dot(
                vector_t[...], inverse[d, :, rows], preferred_element_type=f32
            ).astype(target.dtype)

    first, later = {}, []
    lanes = halves

    def to_near(d):
        i = spots[d]
        back(d + sib, back_near_out.at[i])
        first[d] = send(
            back_near_out.at[i], back_near_in.at[i], back_send.at[i], back_recv.at[i], peer(sib)
        )

    def join(d):
        i = spots[d]
        first[d].wait_recv()
        back_keep[i] = back_keep[i] + back_near_in[i].astype(f32)

    def to_far(d, part, target, slot, device):
        i = spots[d]
        back_far_out[i, :, lanes[part]] = back_keep[i, :, lanes[part]].astype(bf16)
        return send(
            back_far_out.at[i, :, lanes[part]],
            target,
            back_send.at[slot],
            back_recv.at[slot],
            device,
        )

    base = len(spots)
    i = spots[corner]
    corner_near, relayed = [], []

    def corner_near_half(part):
        back(corner + sib, back_near_out.at[i], part)
        slot = i if part == 0 else base + 6
        corner_near.append(
            send(
                back_near_out.at[i, :, lanes[part]],
                back_near_in.at[i, :, lanes[part]],
                back_send.at[slot],
                back_recv.at[slot],
                peer(sib),
            )
        )

    def corner_far_half(part, device):
        corner_near[part].wait_recv()
        back_keep[i, :, lanes[part]] = back_keep[i, :, lanes[part]] + back_near_in[
            i, :, lanes[part]
        ].astype(f32)
        relayed.append(to_far(corner, part, back_relay.at[part], base + part, device))

    corner_near_half(0)
    back(corner, back_keep.at[i], 0)
    corner_near_half(1)
    corner_far_half(0, peer(one))
    back(corner, back_keep.at[i], 1)
    to_near(one)
    corner_far_half(1, peer(two))
    back(one, back_keep.at[spots[one]])
    to_near(two)
    join(one)
    later.append(to_far(one, 0, back_far_in.at[0, :, lanes[0]], base + 2, peer(one)))
    back(two, back_keep.at[spots[two]])
    join(two)
    later.append(to_far(two, 1, back_far_in.at[1, :, lanes[1]], base + 3, peer(two)))
    for d, part, place in ((two, 0, 1), (one, 1, 0)):
        i = spots[d]
        relayed[part].wait_recv()
        back_keep[i, :, lanes[part]] = back_keep[i, :, lanes[part]] + back_relay[part].astype(f32)
        later.append(
            to_far(d, part, back_far_in.at[place, :, lanes[part]], base + 4 + part, peer(d))
        )
    to_near(0)
    back(0, back_keep.at[spots[0]])
    join(0)
    for copy in later:
        copy.wait_recv()
    result = back_keep[spots[0]] + back_far_in[0].astype(f32) + back_far_in[1].astype(f32)
    out[pl.ds(0, local), :] = result.T.astype(bf16)
    for copy in pending:
        copy.wait_send()


def in_one_kernel(
    leaf_rhs,
    leaf_inverse,
    leaf_update,
    root_tiles,
    leaf_dinv,
    leaf_doff,
    leaf_pairs,
    root_rhs,
    root_inverse,
    root_dinv,
    root_doff,
    root_pairs,
):
    f32, bf16 = jnp.float32, jnp.bfloat16
    leaves, tile_count = root_tiles.shape
    group_size = lax.axis_size("leaf") // leaves
    node_count = lax.axis_size("node")
    members = group_size * node_count
    local, rhs = leaf_rhs.shape[1:]
    own_rows, root_rows = root_inverse.shape
    band = members * own_rows
    padded = -(-own_rows // tile_rows) * tile_rows
    half = members // 2
    dma = pltpu.SemaphoreType.DMA
    hbm = pl.BlockSpec(memory_space=pl.ANY)
    vmem = pl.BlockSpec(memory_space=pltpu.VMEM)
    smem = pl.BlockSpec(memory_space=pltpu.SMEM)
    flops = 4 * rhs * (local * members * local + tile_count * tile_rows * local)
    both = pl.pallas_call(
        functools.partial(solve_kernel, leaves, group_size, node_count),
        out_shape=jax.ShapeDtypeStruct((local + own_rows, rhs), bf16),
        in_specs=[hbm, hbm, hbm, smem, vmem, vmem, vmem, vmem, hbm, vmem, vmem, vmem],
        out_specs=vmem,
        scratch_shapes=[
            pltpu.VMEM((members, local, rhs), bf16),
            pltpu.VMEM((members, local, local), bf16),
            pltpu.VMEM((tile_count * tile_rows, local), bf16),
            pltpu.VMEM((padded, root_rows), bf16),
            pltpu.VMEM((local, rhs), f32),
            pltpu.VMEM((local, rhs), bf16),
            pltpu.VMEM((tile_count, tile_rows, rhs), f32),
            pltpu.VMEM((rhs, local), f32),
            pltpu.VMEM((rhs, local), bf16),
            pltpu.VMEM((rhs, tile_count * tile_rows), bf16),
            pltpu.VMEM((root_rows // tile_rows, rhs, tile_rows), f32),
            pltpu.VMEM((2, leaves, band, rhs), f32),
            pltpu.VMEM((2, half, leaves, own_rows, rhs), bf16),
            pltpu.VMEM((2, half, leaves, own_rows, rhs), bf16),
            pltpu.VMEM((2, half, leaves, own_rows, rhs), bf16),
            pltpu.VMEM((2, half, leaves, own_rows, rhs), bf16),
            pltpu.VMEM((2, leaves, own_rows, rhs), bf16),
            pltpu.VMEM((2, leaves, own_rows, rhs), bf16),
            pltpu.VMEM((2, leaves, band, rhs), bf16),
            pltpu.VMEM((half, rhs, local), f32),
            pltpu.VMEM((half, rhs, local), bf16),
            pltpu.VMEM((half, rhs, local), bf16),
            pltpu.VMEM((half, rhs, local), bf16),
            pltpu.VMEM((2, rhs, local), bf16),
            pltpu.VMEM((2, rhs, local // 2), bf16),
            dma((members + 3,)),
            dma((members + 4,)),
            dma((members + 4,)),
            dma((2, leaves * (half + 2))),
            dma((2, leaves * (half + 2))),
            dma((2, leaves * (half + 2))),
            dma((2, leaves * (half + 2))),
            dma((members + 3,)),
            dma((members + 3,)),
        ],
        compiler_params=pltpu.CompilerParams(
            collective_id=0, has_side_effects=True, vmem_limit_bytes=56 * 2**20
        ),
        cost_estimate=pl.CostEstimate(
            flops=flops, bytes_accessed=2 * local * local * members, transcendentals=0
        ),
        name="solve",
    )(
        leaf_rhs,
        leaf_inverse,
        leaf_update,
        root_tiles,
        leaf_dinv,
        leaf_doff,
        leaf_pairs,
        root_rhs,
        root_inverse,
        root_dinv[None],
        root_doff[None],
        root_pairs[None],
    )
    return both[None, :local], both[local:]


def fits_kernel(leaf_rhs, root_tiles, root_rhs, group_size, node_count):
    members = group_size * node_count
    local, own_rows = leaf_rhs.shape[1], root_rhs.shape[0]
    return (
        group_size % 2 == 0
        and members == 8
        and 2 * members * local * local <= 20 * 2**20
        and leaf_rhs.shape[2] == tile_rows
        and local % (2 * tile_rows) == 0
        and own_rows % 16 == 0
        and members * own_rows % tile_rows == 0
    )


def by_shape(*arrays):
    leaf_rhs, root_tiles, root_rhs = arrays[0], arrays[3], arrays[7]
    group_size = lax.axis_size("leaf") // root_tiles.shape[0]
    if fits_kernel(leaf_rhs, root_tiles, root_rhs, group_size, lax.axis_size("node")):
        return in_one_kernel(*arrays)
    return on_device(*arrays)


def solution(mesh):
    in_specs = (
        P("leaf", "node", None),
        P("leaf", "node", None),
        P("leaf", None, "node"),
        P(),
        P("leaf", "node"),
        P("leaf", "node"),
        P("leaf", "node"),
        P(("leaf", "node"), None),
        P(("leaf", "node"), None),
        P(("leaf", "node")),
        P(("leaf", "node")),
        P(("leaf", "node")),
    )
    out_specs = (P("leaf", "node", None), P(("leaf", "node"), None))
    return jax.shard_map(
        by_shape, mesh=mesh, in_specs=in_specs, out_specs=out_specs, check_vma=False
    )
```
